32 devices in a mesh: groups: 2 (over y), ctx: 4 (over z), tp: 4 (over x, core).
Axes of the slice: x: 2, y: 2, z: 4, core: 2. Of those that a mesh axis runs over, the one named last changes fastest.
Arguments:
- inner_gate_proj: bfloat16 [4096, 2048], P('tp', ('groups', 'ctx')), parts along dimension 1, may hold values from -6 to 6
- outer_gate_proj: bfloat16 [4096, 2048], P('tp', ('groups', 'ctx')), parts along dimension 1, may hold values from -6 to 6
- value_projection: bfloat16 [4096, 2048], P('tp', ('groups', 'ctx')), parts along dimension 1, may hold values from -6 to 6
- channel_filter_lags: float32 [4096, 1024], P('tp', 'ctx'), may hold values from -0.1875 to 0.1875
- channel_filter_length: int32 [4096], P('tp'), may hold values from 128 to 1024, as said below
- output_cotangent: bfloat16 [2048, 8192], P(('groups', 'ctx'), 'tp'), parts along dimension 0, may hold values from -6 to 6
- output_weight: bfloat16 [4096, 8192], P('ctx', 'tp'), may hold values from -0.0625 to 0.0625
- adapter_down_factor: bfloat16 [4096, 32], P('tp'), may hold values from -1 to 1
- adapter_up_factor: bfloat16 [32, 8192], P(None, 'tp'), may hold values from -0.0625 to 0.0625
Outputs:
- inner_gate_gradient: bfloat16 [4096, 2048], P('tp', ('groups', 'ctx')), parts along dimension 1
- outer_gate_gradient: bfloat16 [4096, 2048], P('tp', ('groups', 'ctx')), parts along dimension 1
- value_gradient: bfloat16 [4096, 2048], P('tp', ('groups', 'ctx')), parts along dimension 1
- down_factor_gradient: float32 [8192, 32], P(('groups', 'tp')), parts along dimension 0
- up_factor_gradient: float32 [64, 8192], P('groups', 'tp'), parts along dimension 0
The draws below stay inside these ranges and needn't reach their ends.
There are 2 independent parts, one for each index of `groups`. The reference program is written for one: setup_inputs(seed, part) draws one part's arguments, and reference() takes and returns one part's arrays. A program takes and returns all parts, laid end to end along the dimension named above; an argument that names none is the same for every part. Nothing has to cross between parts.
Inputs may be any that keep to these rules, and one draw needn't show every extreme that they name: `channel_filter_length`: equal to 1024 for some channel and to 128 for another.
All inputs are finite; a program needn't handle non-finite values.
Results may differ from the reference program's by a relative error of at most 0.017.
Values may be sent and summed in bfloat16 or wider, within the bound.
A program may use at most 128 MiB of HBM per device.

```python
import math
import jax
import jax.numpy as jnp
from jax import lax

MODEL_WIDTH = 8192
CHANNEL_COUNT = 4096
ADAPTER_RANK = 32
TOKENS = 1024
N_TP = 4


def draw_channel_filter_length(key, part):
    key = jax.random.fold_in(key, 5)
    lengths = jax.random.randint(jax.random.fold_in(key, 1), (CHANNEL_COUNT,), TOKENS // 8, TOKENS + 1)
    place = jax.random.randint(jax.random.fold_in(key, 2), (), 0, CHANNEL_COUNT)
    lengths = lengths.at[place].set(TOKENS)
    lengths = lengths.at[(place + 1) % CHANNEL_COUNT].set(TOKENS // 8)
    return lengths.astype(jnp.int32)


def level_of(own_key, dims, shards, low, largest):
    def one(position, blocks):
        draws = jax.random.uniform(jax.random.fold_in(jax.random.fold_in(own_key, 6), position), (blocks,), jnp.float32, low / len(shards), largest / len(shards))
        return jnp.repeat(jnp.exp(draws), dims[position] // blocks).reshape((-1,) + (1,) * (len(dims) - position - 1))

    factor_of = one(*shards[0])
    for cut in shards[1:]:
        factor_of = factor_of * one(*cut)
    return factor_of


def centred(own_key, dims, scale, most, shards=(), held_as=jnp.bfloat16):
    loudness = level_of(own_key, dims, shards, -0.22, 0.18) if shards else 1.0
    values = jax.random.normal(own_key, dims, jnp.float32) * scale * loudness
    return jnp.minimum(jnp.maximum(values, -most), most).astype(held_as)


def setup_inputs(seed: int = 0, part: int = 0) -> dict:
    streams_of = jax.random.split(jax.random.key(seed), 10)
    part_keys = jax.random.split(jax.random.fold_in(streams_of[9], part), 10)
    return {
        "inner_gate_proj": centred(part_keys[0], (CHANNEL_COUNT, TOKENS), 1.0, 6.0, ((0, 4), (1, 4))),
        "outer_gate_proj": centred(part_keys[1], (CHANNEL_COUNT, TOKENS), 1.0, 6.0, ((0, 4), (1, 4))),
        "value_projection": centred(part_keys[2], (CHANNEL_COUNT, TOKENS), 1.0, 6.0, ((0, 4), (1, 4))),
        "channel_filter_lags": centred(streams_of[3], (CHANNEL_COUNT, TOKENS), TOKENS ** -0.5, 0.1875, ((0, 4), (1, 4)), jnp.float32),
        "channel_filter_length": draw_channel_filter_length(jax.random.fold_in(streams_of[9], 71), part),
        "output_cotangent": centred(part_keys[5], (TOKENS, MODEL_WIDTH), 1.0, 6.0, ((0, 4), (1, 4))),
        "output_weight": centred(streams_of[6], (CHANNEL_COUNT, MODEL_WIDTH), MODEL_WIDTH ** -0.5, 0.0625, ((0, 4), (1, 4))),
        "adapter_down_factor": centred(streams_of[7], (CHANNEL_COUNT, ADAPTER_RANK), ADAPTER_RANK ** -0.5, 1.0, ((0, 4),)),
        "adapter_up_factor": centred(streams_of[8], (ADAPTER_RANK, MODEL_WIDTH), MODEL_WIDTH ** -0.5, 0.0625, ((1, 4),)),
    }


adapter_scale = 2.0


def conv_pair(taps, gated, grad_conv):
    length = taps.shape[1]
    total = 2 * length
    filt_spec = jnp.fft.fft(taps, n=total, axis=1)
    gated_spec = jnp.fft.fft(gated.astype(jnp.float32), n=total, axis=1)
    forward_val = jnp.real(jnp.fft.ifft(filt_spec * gated_spec, axis=1))[:, :length]
    grad_spec = jnp.fft.fft(grad_conv.astype(jnp.float32), n=total, axis=1)
    backward_val = jnp.real(jnp.fft.ifft(jnp.conj(filt_spec) * grad_spec, axis=1))[:, :length]
    return forward_val.astype(jnp.bfloat16), backward_val.astype(jnp.bfloat16)


def product_bf(left, right):
    return (left.astype(jnp.float32) * right.astype(jnp.float32)).astype(jnp.bfloat16)


def reference(inner_gate_proj, outer_gate_proj, value_projection, channel_filter_lags, channel_filter_length, output_cotangent, output_weight, adapter_down_factor, adapter_up_factor):
    lag_index = lax.broadcasted_iota(jnp.int32, (CHANNEL_COUNT, TOKENS), 1)
    masked_filter = jnp.where(lag_index < channel_filter_length[:, None], channel_filter_lags, jnp.zeros_like(channel_filter_lags))
    adapter_backward = lax.dot_general(output_cotangent, adapter_up_factor, (((1,), (1,)), ((), ())), preferred_element_type=jnp.float32)
    width = MODEL_WIDTH // N_TP
    output_backward = jnp.zeros((CHANNEL_COUNT, TOKENS), jnp.float32)
    for shard in range(N_TP):
        term = lax.dot_general(output_weight[:, shard * width:(shard + 1) * width], output_cotangent[:, shard * width:(shard + 1) * width], (((1,), (1,)), ((), ())), preferred_element_type=jnp.float32)
        rounded = lax.optimization_barrier(term.astype(jnp.bfloat16))
        output_backward = output_backward + rounded.astype(jnp.float32)
    projected_gradient = (output_backward + jnp.dot(adapter_down_factor.astype(jnp.float32), adapter_backward.T, precision=lax.Precision.HIGHEST)).astype(jnp.bfloat16)
    gated = product_bf(inner_gate_proj, value_projection)
    grad_conv = product_bf(projected_gradient, outer_gate_proj)
    block = math.gcd(CHANNEL_COUNT, 32)
    shaped = (CHANNEL_COUNT // block, block, TOKENS)
    conv_out, grad_gated = lax.map(lambda items: conv_pair(items[0], items[1], items[2]), (masked_filter.reshape(shaped), gated.reshape(shaped), grad_conv.reshape(shaped)))
    conv_out = conv_out.reshape(CHANNEL_COUNT, TOKENS)
    grad_gated = grad_gated.reshape(CHANNEL_COUNT, TOKENS)
    inner_gate_gradient = product_bf(grad_gated, value_projection)
    value_gradient = product_bf(grad_gated, inner_gate_proj)
    outer_gate_gradient = product_bf(projected_gradient, conv_out)
    block_output = product_bf(outer_gate_proj, conv_out)
    token_adapter_rows = lax.dot_general(block_output, adapter_down_factor, (((0,), (0,)), ((), ())), preferred_element_type=jnp.float32)
    down_factor_gradient = jnp.dot(block_output.astype(jnp.float32), adapter_backward, precision=lax.Precision.HIGHEST) * adapter_scale
    partial_pieces = []
    for shard in range(N_TP):
        column_block = output_cotangent[:, shard * width:(shard + 1) * width].astype(jnp.float32)
        partial_pieces.append(lax.dot_general(token_adapter_rows, column_block, (((0,), (0,)), ((), ())), precision=lax.Precision.HIGHEST))
    up_factor_gradient = jnp.concatenate(partial_pieces, axis=1) * adapter_scale
    return inner_gate_gradient, outer_gate_gradient, value_gradient, down_factor_gradient, up_factor_gradient
```

```python
import math

import jax
import jax.numpy as jnp
import ml_dtypes
import numpy as np
from jax import lax
from jax.sharding import PartitionSpec as P

adapter_scale = 2.0


def product_bf(left, right):
    return (left.astype(jnp.float32) * right.astype(jnp.float32)).astype(jnp.bfloat16)


def dft_table(length):
    across = lax.broadcasted_iota(jnp.int32, (length, length), 0)
    downward = lax.broadcasted_iota(jnp.int32, (length, length), 1)
    angle = -2.0 * math.pi / length * (across * downward % length).astype(jnp.float32)
    return (jnp.cos(angle), jnp.sin(angle))


def twiddle_table(outer, inner):
    total = outer * inner
    first_idx = lax.broadcasted_iota(jnp.int32, (outer, inner), 0)
    second_idx = lax.broadcasted_iota(jnp.int32, (outer, inner), 1)
    angle = -2.0 * math.pi / total * (first_idx * second_idx % total).astype(jnp.float32)
    return (jnp.cos(angle), jnp.sin(angle))


def left_apply(table, field):
    return jnp.einsum("ap,cpq->caq", table, field, precision=lax.Precision.HIGHEST)


def right_apply(field, table):
    return jnp.einsum("caq,qb->cab", field, table, precision=lax.Precision.HIGHEST)


def forward_dft(signal, tables):
    outer_cos, outer_sin, inner_cos, inner_sin, twist_cos, twist_sin = tables
    channels = signal.shape[0]
    block = signal.reshape(channels, outer_cos.shape[0], inner_cos.shape[0])
    first_real = left_apply(outer_cos, block)
    first_imag = left_apply(outer_sin, block)
    turned_real = first_real * twist_cos - first_imag * twist_sin
    turned_imag = first_real * twist_sin + first_imag * twist_cos
    spec_real = right_apply(turned_real, inner_cos) - right_apply(turned_imag, inner_sin)
    spec_imag = right_apply(turned_real, inner_sin) + right_apply(turned_imag, inner_cos)
    return (spec_real, spec_imag)


def inverse_real(spec_real, spec_imag, tables):
    outer_cos, outer_sin, inner_cos, inner_sin, twist_cos, twist_sin = tables
    back_real = right_apply(spec_real, inner_cos) + right_apply(spec_imag, inner_sin)
    back_imag = right_apply(spec_imag, inner_cos) - right_apply(spec_real, inner_sin)
    untwist_real = back_real * twist_cos + back_imag * twist_sin
    untwist_imag = back_imag * twist_cos - back_real * twist_sin
    result = left_apply(outer_cos, untwist_real) + left_apply(outer_sin, untwist_imag)
    total = outer_cos.shape[0] * inner_cos.shape[0]
    return result.reshape(result.shape[0], total) / total


def convolve(taps, gated, grad_conv):
    channels, length = taps.shape
    total = 2 * length
    outer = 1 << (total.bit_length() - 1) // 2
    inner = total // outer
    outer_cos, outer_sin = dft_table(outer)
    inner_cos, inner_sin = dft_table(inner)
    twist_cos, twist_sin = twiddle_table(outer, inner)
    tables = (outer_cos, outer_sin, inner_cos, inner_sin, twist_cos, twist_sin)
    padding = jnp.zeros((channels, length), jnp.float32)

    def spectrum(field):
        return forward_dft(jnp.concatenate([field.astype(jnp.float32), padding], axis=1), tables)

    filt_real, filt_imag = spectrum(taps)
    gated_real, gated_imag = spectrum(gated)
    grad_real, grad_imag = spectrum(grad_conv)
    forward_val = inverse_real(
        filt_real * gated_real - filt_imag * gated_imag,
        filt_real * gated_imag + filt_imag * gated_real,
        tables,
    )[:, :length]
    backward_val = inverse_real(
        filt_real * grad_real + filt_imag * grad_imag,
        filt_real * grad_imag - filt_imag * grad_real,
        tables,
    )[:, :length]
    return (forward_val.astype(jnp.bfloat16), backward_val.astype(jnp.bfloat16))


dense_length = 2048


def dense_table(length):
    lag = np.arange(length, dtype=np.int64)[:, None]
    freq = np.arange(length, dtype=np.int64)[None, :]
    angle = np.pi / (2 * length) * (lag * (2 * freq + 1) % (4 * length))
    table = np.concatenate([np.cos(angle), np.sin(angle)], axis=1)
    return jnp.asarray(table.astype(ml_dtypes.bfloat16))


def dense_spectrum(field, table):
    spec = jnp.dot(field, table, preferred_element_type=jnp.float32)
    return spec[:, : field.shape[1]], spec[:, field.shape[1] :]


def dense_inverse(cos_part, sin_part, table):
    spec = jnp.concatenate([cos_part, sin_part], axis=1).astype(jnp.bfloat16)
    field = lax.dot_general(
        spec, table, (((1,), (1,)), ((), ())), preferred_element_type=jnp.float32
    )
    return (field * (1.0 / table.shape[0])).astype(jnp.bfloat16)


def convolve_dense(taps, gated, grad_conv):
    table = dense_table(taps.shape[1])
    filt_cos, filt_sin = dense_spectrum(taps, table)
    gated_cos, gated_sin = dense_spectrum(gated, table)
    conv = dense_inverse(
        filt_cos * gated_cos - filt_sin * gated_sin,
        filt_cos * gated_sin + filt_sin * gated_cos,
        table,
    )
    grad_cos, grad_sin = dense_spectrum(grad_conv, table)
    back = dense_inverse(
        filt_cos * grad_cos + filt_sin * grad_sin,
        filt_cos * grad_sin - filt_sin * grad_cos,
        table,
    )
    return conv, back


def local(
    inner_gate_proj,
    outer_gate_proj,
    value_projection,
    channel_filter_lags,
    channel_filter_length,
    output_cotangent,
    output_weight,
    adapter_down_factor,
    adapter_up_factor,
):
    ctx_size, tp_size = lax.axis_size("ctx"), lax.axis_size("tp")
    tok_rows = inner_gate_proj.shape[1]
    lag_index = lax.axis_index("ctx") * tok_rows + lax.broadcasted_iota(
        jnp.int32, channel_filter_lags.shape, 1
    )
    masked_filter = jnp.where(
        lag_index < channel_filter_length[:, None],
        channel_filter_lags,
        jnp.zeros_like(channel_filter_lags),
    ).astype(jnp.bfloat16)
    gated = product_bf(inner_gate_proj, value_projection)
    whole_cotangent = lax.all_gather(output_cotangent, "ctx", axis=0, tiled=True)
    filter_ch, gated_ch, outer_ch = lax.all_to_all(
        jnp.stack([masked_filter, gated, outer_gate_proj]),
        "ctx",
        split_axis=1,
        concat_axis=2,
        tiled=True,
    )
    rows = filter_ch.shape[0]
    down_rows = lax.dynamic_slice_in_dim(
        adapter_down_factor, lax.axis_index("ctx") * rows, rows, axis=0
    )
    partial = lax.dot_general(
        output_weight,
        whole_cotangent,
        (((1,), (1,)), ((), ())),
        preferred_element_type=jnp.float32,
    ).astype(jnp.bfloat16)
    adapter_backward = lax.psum(
        lax.dot_general(
            whole_cotangent,
            adapter_up_factor,
            (((1,), (1,)), ((), ())),
            preferred_element_type=jnp.float32,
        ).astype(jnp.bfloat16),
        "tp",
    )
    scattered = lax.psum_scatter(partial, "tp", scatter_dimension=0, tiled=True)
    moves = [(i, (i % ctx_size) * tp_size + i // ctx_size) for i in range(ctx_size * tp_size)]
    output_backward = lax.ppermute(scattered, ("ctx", "tp"), moves).astype(jnp.float32)
    adapter_term = lax.dot_general(
        down_rows,
        adapter_backward,
        (((1,), (1,)), ((), ())),
        preferred_element_type=jnp.float32,
    )
    projected_gradient = (output_backward + adapter_term).astype(jnp.bfloat16)
    grad_conv = product_bf(projected_gradient, outer_ch)
    if filter_ch.shape[1] <= dense_length:
        conv_ch, grad_gated_ch = convolve_dense(filter_ch, gated_ch, grad_conv)
    else:
        conv_ch, grad_gated_ch = convolve(filter_ch.astype(jnp.float32), gated_ch, grad_conv)
    block_output = product_bf(outer_ch, conv_ch)
    token_part = lax.dot_general(
        block_output,
        down_rows,
        (((0,), (0,)), ((), ())),
        preferred_element_type=jnp.float32,
    )
    token_adapter = lax.psum(token_part.astype(jnp.bfloat16), ("ctx", "tp"))
    outer_grad_ch = product_bf(projected_gradient, conv_ch)
    grad_gated, outer_gate_gradient = lax.all_to_all(
        jnp.stack([grad_gated_ch, outer_grad_ch]),
        "ctx",
        split_axis=2,
        concat_axis=1,
        tiled=True,
    )
    down_part = jnp.dot(block_output, adapter_backward, preferred_element_type=jnp.float32)
    down_sum = lax.all_gather(down_part.astype(jnp.bfloat16), "ctx", axis=0, tiled=True)
    up_sum = lax.dot_general(
        token_adapter,
        whole_cotangent,
        (((0,), (0,)), ((), ())),
        preferred_element_type=jnp.float32,
    )
    return (
        product_bf(grad_gated, value_projection),
        outer_gate_gradient,
        product_bf(grad_gated, inner_gate_proj),
        down_sum.astype(jnp.float32) * adapter_scale,
        up_sum * adapter_scale,
    )


def solution(mesh):
    return jax.shard_map(
        local,
        mesh=mesh,
        in_specs=(
            P("tp", ("groups", "ctx")),
            P("tp", ("groups", "ctx")),
            P("tp", ("groups", "ctx")),
            P("tp", "ctx"),
            P("tp"),
            P(("groups", "ctx"), "tp"),
            P("ctx", "tp"),
            P("tp", None),
            P(None, "tp"),
        ),
        out_specs=(
            P("tp", ("groups", "ctx")),
            P("tp", ("groups", "ctx")),
            P("tp", ("groups", "ctx")),
            P(("groups", "tp"), None),
            P("groups", "tp"),
        ),
        check_vma=False,
    )
```

```python
import functools
import math

import jax
import jax.numpy as jnp
import ml_dtypes
import numpy as np
from jax import lax
from jax.experimental import pallas as pl
from jax.experimental.pallas import tpu as pltpu
from jax.sharding import PartitionSpec as P

adapter_scale = 2.0


def product_bf(left, right):
    return (left.astype(jnp.float32) * right.astype(jnp.float32)).astype(jnp.bfloat16)


def dft_table(length):
    across = lax.broadcasted_iota(jnp.int32, (length, length), 0)
    downward = lax.broadcasted_iota(jnp.int32, (length, length), 1)
    angle = -2.0 * math.pi / length * (across * downward % length).astype(jnp.float32)
    return (jnp.cos(angle), jnp.sin(angle))


def twiddle_table(outer, inner):
    total = outer * inner
    first_idx = lax.broadcasted_iota(jnp.int32, (outer, inner), 0)
    second_idx = lax.broadcasted_iota(jnp.int32, (outer, inner), 1)
    angle = -2.0 * math.pi / total * (first_idx * second_idx % total).astype(jnp.float32)
    return (jnp.cos(angle), jnp.sin(angle))


def left_apply(table, field):
    return jnp.einsum("ap,cpq->caq", table, field, precision=lax.Precision.HIGHEST)


def right_apply(field, table):
    return jnp.einsum("caq,qb->cab", field, table, precision=lax.Precision.HIGHEST)


def forward_dft(signal, tables):
    outer_cos, outer_sin, inner_cos, inner_sin, twist_cos, twist_sin = tables
    channels = signal.shape[0]
    block = signal.reshape(channels, outer_cos.shape[0], inner_cos.shape[0])
    first_real = left_apply(outer_cos, block)
    first_imag = left_apply(outer_sin, block)
    turned_real = first_real * twist_cos - first_imag * twist_sin
    turned_imag = first_real * twist_sin + first_imag * twist_cos
    spec_real = right_apply(turned_real, inner_cos) - right_apply(turned_imag, inner_sin)
    spec_imag = right_apply(turned_real, inner_sin) + right_apply(turned_imag, inner_cos)
    return (spec_real, spec_imag)


def inverse_real(spec_real, spec_imag, tables):
    outer_cos, outer_sin, inner_cos, inner_sin, twist_cos, twist_sin = tables
    back_real = right_apply(spec_real, inner_cos) + right_apply(spec_imag, inner_sin)
    back_imag = right_apply(spec_imag, inner_cos) - right_apply(spec_real, inner_sin)
    untwist_real = back_real * twist_cos + back_imag * twist_sin
    untwist_imag = back_imag * twist_cos - back_real * twist_sin
    result = left_apply(outer_cos, untwist_real) + left_apply(outer_sin, untwist_imag)
    total = outer_cos.shape[0] * inner_cos.shape[0]
    return result.reshape(result.shape[0], total) / total


def convolve(taps, gated, grad_conv):
    channels, length = taps.shape
    total = 2 * length
    outer = 1 << (total.bit_length() - 1) // 2
    inner = total // outer
    outer_cos, outer_sin = dft_table(outer)
    inner_cos, inner_sin = dft_table(inner)
    twist_cos, twist_sin = twiddle_table(outer, inner)
    tables = (outer_cos, outer_sin, inner_cos, inner_sin, twist_cos, twist_sin)
    padding = jnp.zeros((channels, length), jnp.float32)

    def spectrum(field):
        return forward_dft(jnp.concatenate([field.astype(jnp.float32), padding], axis=1), tables)

    filt_real, filt_imag = spectrum(taps)
    gated_real, gated_imag = spectrum(gated)
    grad_real, grad_imag = spectrum(grad_conv)
    forward_val = inverse_real(
        filt_real * gated_real - filt_imag * gated_imag,
        filt_real * gated_imag + filt_imag * gated_real,
        tables,
    )[:, :length]
    backward_val = inverse_real(
        filt_real * grad_real + filt_imag * grad_imag,
        filt_real * grad_imag - filt_imag * grad_real,
        tables,
    )[:, :length]
    return (forward_val.astype(jnp.bfloat16), backward_val.astype(jnp.bfloat16))


dense_length = 2048


def dense_table(length):
    lag = np.arange(length, dtype=np.int64)[:, None]
    freq = np.arange(length, dtype=np.int64)[None, :]
    angle = np.pi / (2 * length) * (lag * (2 * freq + 1) % (4 * length))
    table = np.concatenate([np.cos(angle), np.sin(angle)], axis=1)
    return jnp.asarray(table.astype(ml_dtypes.bfloat16))


def dense_spectrum(field, table):
    spec = jnp.dot(field, table, preferred_element_type=jnp.float32)
    return spec[:, : field.shape[1]], spec[:, field.shape[1] :]


def dense_inverse(cos_part, sin_part, table):
    spec = jnp.concatenate([cos_part, sin_part], axis=1).astype(jnp.bfloat16)
    field = lax.dot_general(
        spec, table, (((1,), (1,)), ((), ())), preferred_element_type=jnp.float32
    )
    return (field * (1.0 / table.shape[0])).astype(jnp.bfloat16)


def convolve_dense(taps, gated, grad_conv):
    table = dense_table(taps.shape[1])
    filt_cos, filt_sin = dense_spectrum(taps, table)
    gated_cos, gated_sin = dense_spectrum(gated, table)
    conv = dense_inverse(
        filt_cos * gated_cos - filt_sin * gated_sin,
        filt_cos * gated_sin + filt_sin * gated_cos,
        table,
    )
    grad_cos, grad_sin = dense_spectrum(grad_conv, table)
    back = dense_inverse(
        filt_cos * grad_cos + filt_sin * grad_sin,
        filt_cos * grad_sin - filt_sin * grad_cos,
        table,
    )
    return conv, back


kernel_peers = 16


def position():
    ctx_size, tp_size = lax.axis_size("ctx"), lax.axis_size("tp")
    count = ctx_size * tp_size
    me = lax.axis_index("ctx") * tp_size + lax.axis_index("tp")

    def peer(step):
        other = lax.rem(me + step, count)
        return {"ctx": other // tp_size, "tp": lax.rem(other, tp_size)}

    return me, count, peer


def greet(count, peer):
    barrier = pltpu.get_barrier_semaphore()
    for step in range(1, count):
        pl.semaphore_signal(
            barrier, inc=1, device_id=peer(step), device_id_type=pl.DeviceIdType.MESH
        )
    pl.semaphore_wait(barrier, count - 1)


def push(src, dst, send_sem, recv_sem, device):
    copy = pltpu.make_async_remote_copy(
        src_ref=src,
        dst_ref=dst,
        send_sem=send_sem,
        recv_sem=recv_sem,
        device_id=device,
        device_id_type=pl.DeviceIdType.MESH,
    )
    copy.start()
    return copy


def return_kernel(
    ctx_size,
    tp_size,
    grad_ref,
    outer_ref,
    token_ref,
    down_ref,
    cotangent_ref,
    grad_out,
    outer_out,
    down_out,
    up_out,
    parts,
    whole,
    send_tok,
    recv_tok,
    send_all,
    recv_all,
    send_row,
    recv_row,
    local_sem,
):
    me, count, peer = position()
    ctx, tp = lax.axis_index("ctx"), lax.axis_index("tp")
    rows, length = grad_ref.shape
    width = length // ctx_size
    lanes = length // 128
    greet(count, peer)

    def chunk(ref, place):
        top = pl.multiple_of(place // lanes * 16, 16)
        left = pl.multiple_of(lax.rem(place, lanes) * 128, 128)
        return ref.at[pl.ds(top, 16), pl.ds(left, 128)]

    copies = []
    for step in range(1, count):
        copies.append(
            push(
                chunk(token_ref, lax.rem(me + step, count)),
                parts.at[step],
                send_tok.at[step],
                recv_tok.at[step],
                peer(step),
            )
        )
    my_rows = pl.ds(pl.multiple_of(ctx * rows, 16), rows)
    my_cols = pl.ds(pl.multiple_of(ctx * width, 128), width)
    my_lags = pl.ds(pl.multiple_of(ctx * rows, 128), rows)
    later = []
    for step in range(1, ctx_size):
        other = lax.rem(ctx + step, ctx_size)
        device = {"ctx": other, "tp": tp}
        cols = pl.ds(pl.multiple_of(other * width, 128), width)
        moves = (
            (down_ref, down_out.at[:, my_lags]),
            (grad_ref.at[:, cols], grad_out.at[my_rows, :]),
            (outer_ref.at[:, cols], outer_out.at[my_rows, :]),
        )
        for kind, (src, dst) in enumerate(moves):
            later.append(push(src, dst, send_row.at[kind, step], recv_row.at[kind, step], device))
    down_out[:, my_lags] = down_ref[...]
    grad_out[my_rows, :] = grad_ref[:, my_cols]
    outer_out[my_rows, :] = outer_ref[:, my_cols]

    own = pltpu.make_async_copy(chunk(token_ref, me), parts.at[0], local_sem)
    own.start()
    own.wait()
    total = parts[0].astype(jnp.float32)
    for step in range(1, count):
        copies[step - 1].wait_recv()
        total += parts[step].astype(jnp.float32)
    for copy in copies:
        copy.wait_send()
    parts[0] = total.astype(jnp.bfloat16)
    copies = []
    for step in range(1, count):
        copies.append(
            push(
                parts.at[0],
                chunk(whole, me),
                send_all.at[step],
                recv_all.at[step],
                peer(step),
            )
        )
    own = pltpu.make_async_copy(parts.at[0], chunk(whole, me), local_sem)
    own.start()
    own.wait()
    for copy in copies:
        copy.wait()
    up_out[...] = adapter_scale * jnp.dot(
        whole[...], cotangent_ref[...], preferred_element_type=jnp.float32
    )
    for copy in later:
        copy.wait()


def return_all(grad_gated_ch, outer_grad_ch, token_t, down_t, whole_cotangent):
    ctx_size, tp_size = lax.axis_size("ctx"), lax.axis_size("tp")
    count = ctx_size * tp_size
    rows, length = grad_gated_ch.shape
    rank = token_t.shape[0]
    tokens = jax.ShapeDtypeStruct((rows * ctx_size, length // ctx_size), jnp.bfloat16)
    dma = pltpu.SemaphoreType.DMA
    return pl.pallas_call(
        functools.partial(return_kernel, ctx_size, tp_size),
        out_shape=(
            tokens,
            tokens,
            jax.ShapeDtypeStruct((rank, rows * ctx_size), jnp.bfloat16),
            jax.ShapeDtypeStruct((rank, whole_cotangent.shape[1]), jnp.float32),
        ),
        in_specs=[pl.BlockSpec(memory_space=pltpu.VMEM)] * 5,
        out_specs=(pl.BlockSpec(memory_space=pltpu.VMEM),) * 4,
        scratch_shapes=[
            pltpu.VMEM((count, 16, 128), jnp.bfloat16),
            pltpu.VMEM((rank, length), jnp.bfloat16),
            dma((count,)),
            dma((count,)),
            dma((count,)),
            dma((count,)),
            dma((3, ctx_size)),
            dma((3, ctx_size)),
            dma,
        ],
        compiler_params=pltpu.CompilerParams(
            collective_id=1, has_side_effects=True, vmem_limit_bytes=40 << 20
        ),
    )(grad_gated_ch, outer_grad_ch, token_t, down_t, whole_cotangent)


def token_by_kernel(count, shape, rank):
    return count <= kernel_peers and shape[1] <= dense_length and rank * shape[1] == count * 2048


def local(
    inner_gate_proj,
    outer_gate_proj,
    value_projection,
    channel_filter_lags,
    channel_filter_length,
    output_cotangent,
    output_weight,
    adapter_down_factor,
    adapter_up_factor,
):
    ctx_size, tp_size = lax.axis_size("ctx"), lax.axis_size("tp")
    tok_rows = inner_gate_proj.shape[1]
    lag_index = lax.axis_index("ctx") * tok_rows + lax.broadcasted_iota(
        jnp.int32, channel_filter_lags.shape, 1
    )
    masked_filter = jnp.where(
        lag_index < channel_filter_length[:, None],
        channel_filter_lags,
        jnp.zeros_like(channel_filter_lags),
    ).astype(jnp.bfloat16)
    gated = product_bf(inner_gate_proj, value_projection)
    whole_cotangent = lax.all_gather(output_cotangent, "ctx", axis=0, tiled=True)
    filter_ch, gated_ch, outer_ch = lax.all_to_all(
        jnp.stack([masked_filter, gated, outer_gate_proj]),
        "ctx",
        split_axis=1,
        concat_axis=2,
        tiled=True,
    )
    rows = filter_ch.shape[0]
    down_rows = lax.dynamic_slice_in_dim(
        adapter_down_factor, lax.axis_index("ctx") * rows, rows, axis=0
    )
    partial = lax.dot_general(
        output_weight,
        whole_cotangent,
        (((1,), (1,)), ((), ())),
        preferred_element_type=jnp.float32,
    ).astype(jnp.bfloat16)
    adapter_backward = lax.psum(
        lax.dot_general(
            whole_cotangent,
            adapter_up_factor,
            (((1,), (1,)), ((), ())),
            preferred_element_type=jnp.float32,
        ).astype(jnp.bfloat16),
        "tp",
    )
    scattered = lax.psum_scatter(partial, "tp", scatter_dimension=0, tiled=True)
    moves = [(i, (i % ctx_size) * tp_size + i // ctx_size) for i in range(ctx_size * tp_size)]
    output_backward = lax.ppermute(scattered, ("ctx", "tp"), moves).astype(jnp.float32)
    adapter_term = lax.dot_general(
        down_rows,
        adapter_backward,
        (((1,), (1,)), ((), ())),
        preferred_element_type=jnp.float32,
    )
    projected_gradient = (output_backward + adapter_term).astype(jnp.bfloat16)
    grad_conv = product_bf(projected_gradient, outer_ch)
    if filter_ch.shape[1] <= dense_length:
        conv_ch, grad_gated_ch = convolve_dense(filter_ch, gated_ch, grad_conv)
    else:
        conv_ch, grad_gated_ch = convolve(filter_ch.astype(jnp.float32), gated_ch, grad_conv)
    block_output = product_bf(outer_ch, conv_ch)
    outer_grad_ch = product_bf(projected_gradient, conv_ch)
    if token_by_kernel(ctx_size * tp_size, filter_ch.shape, adapter_down_factor.shape[1]):
        token_t = lax.dot_general(
            down_rows,
            block_output,
            (((0,), (0,)), ((), ())),
            preferred_element_type=jnp.float32,
        ).astype(jnp.bfloat16)
        down_t = lax.dot_general(
            adapter_backward,
            block_output,
            (((0,), (1,)), ((), ())),
            preferred_element_type=jnp.float32,
        ).astype(jnp.bfloat16)
        grad_gated, outer_gate_gradient, down_sum, up_sum = return_all(
            grad_gated_ch, outer_grad_ch, token_t, down_t, whole_cotangent
        )
        return (
            product_bf(grad_gated, value_projection),
            outer_gate_gradient,
            product_bf(grad_gated, inner_gate_proj),
            down_sum.astype(jnp.float32).T * adapter_scale,
            up_sum,
        )
    token_part = lax.dot_general(
        block_output,
        down_rows,
        (((0,), (0,)), ((), ())),
        preferred_element_type=jnp.float32,
    )
    token_adapter = lax.psum(token_part.astype(jnp.bfloat16), ("ctx", "tp"))
    grad_gated, outer_gate_gradient = lax.all_to_all(
        jnp.stack([grad_gated_ch, outer_grad_ch]),
        "ctx",
        split_axis=2,
        concat_axis=1,
        tiled=True,
    )
    down_part = jnp.dot(block_output, adapter_backward, preferred_element_type=jnp.float32)
    down_sum = lax.all_gather(down_part.astype(jnp.bfloat16), "ctx", axis=0, tiled=True)
    up_sum = lax.dot_general(
        token_adapter,
        whole_cotangent,
        (((0,), (0,)), ((), ())),
        preferred_element_type=jnp.float32,
    )
    return (
        product_bf(grad_gated, value_projection),
        outer_gate_gradient,
        product_bf(grad_gated, inner_gate_proj),
        down_sum.astype(jnp.float32) * adapter_scale,
        up_sum * adapter_scale,
    )


def solution(mesh):
    return jax.shard_map(
        local,
        mesh=mesh,
        in_specs=(
            P("tp", ("groups", "ctx")),
            P("tp", ("groups", "ctx")),
            P("tp", ("groups", "ctx")),
            P("tp", "ctx"),
            P("tp"),
            P(("groups", "ctx"), "tp"),
            P("ctx", "tp"),
            P("tp", None),
            P(None, "tp"),
        ),
        out_specs=(
            P("tp", ("groups", "ctx")),
            P("tp", ("groups", "ctx")),
            P("tp", ("groups", "ctx")),
            P(("groups", "tp"), None),
            P("groups", "tp"),
        ),
        check_vma=False,
    )
```

```python
import functools
import math

import jax
import jax.numpy as jnp
import ml_dtypes
import numpy as np
from jax import lax
from jax.experimental import pallas as pl
from jax.experimental.pallas import tpu as pltpu
from jax.sharding import PartitionSpec as P

adapter_scale = 2.0


def product_bf(left, right):
    return (left.astype(jnp.float32) * right.astype(jnp.float32)).astype(jnp.bfloat16)


def dft_table(length):
    across = lax.broadcasted_iota(jnp.int32, (length, length), 0)
    downward = lax.broadcasted_iota(jnp.int32, (length, length), 1)
    angle = -2.0 * math.pi / length * (across * downward % length).astype(jnp.float32)
    return (jnp.cos(angle), jnp.sin(angle))


def twiddle_table(outer, inner):
    total = outer * inner
    first_idx = lax.broadcasted_iota(jnp.int32, (outer, inner), 0)
    second_idx = lax.broadcasted_iota(jnp.int32, (outer, inner), 1)
    angle = -2.0 * math.pi / total * (first_idx * second_idx % total).astype(jnp.float32)
    return (jnp.cos(angle), jnp.sin(angle))


def left_apply(table, field):
    return jnp.einsum("ap,cpq->caq", table, field, precision=lax.Precision.HIGHEST)


def right_apply(field, table):
    return jnp.einsum("caq,qb->cab", field, table, precision=lax.Precision.HIGHEST)


def forward_dft(signal, tables):
    outer_cos, outer_sin, inner_cos, inner_sin, twist_cos, twist_sin = tables
    channels = signal.shape[0]
    block = signal.reshape(channels, outer_cos.shape[0], inner_cos.shape[0])
    first_real = left_apply(outer_cos, block)
    first_imag = left_apply(outer_sin, block)
    turned_real = first_real * twist_cos - first_imag * twist_sin
    turned_imag = first_real * twist_sin + first_imag * twist_cos
    spec_real = right_apply(turned_real, inner_cos) - right_apply(turned_imag, inner_sin)
    spec_imag = right_apply(turned_real, inner_sin) + right_apply(turned_imag, inner_cos)
    return (spec_real, spec_imag)


def inverse_real(spec_real, spec_imag, tables):
    outer_cos, outer_sin, inner_cos, inner_sin, twist_cos, twist_sin = tables
    back_real = right_apply(spec_real, inner_cos) + right_apply(spec_imag, inner_sin)
    back_imag = right_apply(spec_imag, inner_cos) - right_apply(spec_real, inner_sin)
    untwist_real = back_real * twist_cos + back_imag * twist_sin
    untwist_imag = back_imag * twist_cos - back_real * twist_sin
    result = left_apply(outer_cos, untwist_real) + left_apply(outer_sin, untwist_imag)
    total = outer_cos.shape[0] * inner_cos.shape[0]
    return result.reshape(result.shape[0], total) / total


def convolve(taps, gated, grad_conv):
    channels, length = taps.shape
    total = 2 * length
    outer = 1 << (total.bit_length() - 1) // 2
    inner = total // outer
    outer_cos, outer_sin = dft_table(outer)
    inner_cos, inner_sin = dft_table(inner)
    twist_cos, twist_sin = twiddle_table(outer, inner)
    tables = (outer_cos, outer_sin, inner_cos, inner_sin, twist_cos, twist_sin)
    padding = jnp.zeros((channels, length), jnp.float32)

    def spectrum(field):
        return forward_dft(jnp.concatenate([field.astype(jnp.float32), padding], axis=1), tables)

    filt_real, filt_imag = spectrum(taps)
    gated_real, gated_imag = spectrum(gated)
    grad_real, grad_imag = spectrum(grad_conv)
    forward_val = inverse_real(
        filt_real * gated_real - filt_imag * gated_imag,
        filt_real * gated_imag + filt_imag * gated_real,
        tables,
    )[:, :length]
    backward_val = inverse_real(
        filt_real * grad_real + filt_imag * grad_imag,
        filt_real * grad_imag - filt_imag * grad_real,
        tables,
    )[:, :length]
    return (forward_val.astype(jnp.bfloat16), backward_val.astype(jnp.bfloat16))


dense_length = 2048


def dense_table(length):
    lag = np.arange(length, dtype=np.int64)[:, None]
    freq = np.arange(length, dtype=np.int64)[None, :]
    angle = np.pi / (2 * length) * (lag * (2 * freq + 1) % (4 * length))
    table = np.concatenate([np.cos(angle), np.sin(angle)], axis=1)
    return jnp.asarray(table.astype(ml_dtypes.bfloat16))


def dense_spectrum(field, table):
    spec = jnp.dot(field, table, preferred_element_type=jnp.float32)
    return spec[:, : field.shape[1]], spec[:, field.shape[1] :]


def dense_inverse(cos_part, sin_part, table):
    spec = jnp.concatenate([cos_part, sin_part], axis=1).astype(jnp.bfloat16)
    field = lax.dot_general(
        spec, table, (((1,), (1,)), ((), ())), preferred_element_type=jnp.float32
    )
    return (field * (1.0 / table.shape[0])).astype(jnp.bfloat16)


def convolve_dense(taps, gated, grad_conv):
    table = dense_table(taps.shape[1])
    filt_cos, filt_sin = dense_spectrum(taps, table)
    gated_cos, gated_sin = dense_spectrum(gated, table)
    conv = dense_inverse(
        filt_cos * gated_cos - filt_sin * gated_sin,
        filt_cos * gated_sin + filt_sin * gated_cos,
        table,
    )
    grad_cos, grad_sin = dense_spectrum(grad_conv, table)
    back = dense_inverse(
        filt_cos * grad_cos + filt_sin * grad_sin,
        filt_cos * grad_sin - filt_sin * grad_cos,
        table,
    )
    return conv, back


kernel_peers = 16


def position():
    ctx_size, tp_size = lax.axis_size("ctx"), lax.axis_size("tp")
    count = ctx_size * tp_size
    me = lax.axis_index("ctx") * tp_size + lax.axis_index("tp")

    def peer(step):
        other = lax.rem(me + step, count)
        return {"ctx": other // tp_size, "tp": lax.rem(other, tp_size)}

    return me, count, peer


def greet(count, peer):
    barrier = pltpu.get_barrier_semaphore()
    for step in range(1, count):
        pl.semaphore_signal(
            barrier, inc=1, device_id=peer(step), device_id_type=pl.DeviceIdType.MESH
        )
    pl.semaphore_wait(barrier, count - 1)


def push(src, dst, send_sem, recv_sem, device):
    copy = pltpu.make_async_remote_copy(
        src_ref=src,
        dst_ref=dst,
        send_sem=send_sem,
        recv_sem=recv_sem,
        device_id=device,
        device_id_type=pl.DeviceIdType.MESH,
    )
    copy.start()
    return copy


def return_kernel(
    ctx_size,
    tp_size,
    grad_ref,
    outer_ref,
    token_ref,
    down_ref,
    cotangent_ref,
    grad_out,
    outer_out,
    down_out,
    up_out,
    parts,
    whole,
    send_tok,
    recv_tok,
    send_all,
    recv_all,
    send_row,
    recv_row,
    local_sem,
):
    me, count, peer = position()
    ctx, tp = lax.axis_index("ctx"), lax.axis_index("tp")
    rows, length = grad_ref.shape
    width = length // ctx_size
    lanes = length // 128
    greet(count, peer)

    def chunk(ref, place):
        top = pl.multiple_of(place // lanes * 16, 16)
        left = pl.multiple_of(lax.rem(place, lanes) * 128, 128)
        return ref.at[pl.ds(top, 16), pl.ds(left, 128)]

    copies = []
    for step in range(1, count):
        copies.append(
            push(
                chunk(token_ref, lax.rem(me + step, count)),
                parts.at[step],
                send_tok.at[step],
                recv_tok.at[step],
                peer(step),
            )
        )
    my_rows = pl.ds(pl.multiple_of(ctx * rows, 16), rows)
    my_cols = pl.ds(pl.multiple_of(ctx * width, 128), width)
    my_lags = pl.ds(pl.multiple_of(ctx * rows, 128), rows)
    later = []
    for step in range(1, ctx_size):
        other = lax.rem(ctx + step, ctx_size)
        device = {"ctx": other, "tp": tp}
        cols = pl.ds(pl.multiple_of(other * width, 128), width)
        moves = (
            (down_ref, down_out.at[:, my_lags]),
            (grad_ref.at[:, cols], grad_out.at[my_rows, :]),
            (outer_ref.at[:, cols], outer_out.at[my_rows, :]),
        )
        for kind, (src, dst) in enumerate(moves):
            later.append(push(src, dst, send_row.at[kind, step], recv_row.at[kind, step], device))
    down_out[:, my_lags] = down_ref[...]
    grad_out[my_rows, :] = grad_ref[:, my_cols]
    outer_out[my_rows, :] = outer_ref[:, my_cols]

    own = pltpu.make_async_copy(chunk(token_ref, me), parts.at[0], local_sem)
    own.start()
    own.wait()
    total = parts[0].astype(jnp.float32)
    for step in range(1, count):
        copies[step - 1].wait_recv()
        total += parts[step].astype(jnp.float32)
    for copy in copies:
        copy.wait_send()
    parts[0] = total.astype(jnp.bfloat16)
    copies = []
    for step in range(1, count):
        copies.append(
            push(
                parts.at[0],
                chunk(whole, me),
                send_all.at[step],
                recv_all.at[step],
                peer(step),
            )
        )
    own = pltpu.make_async_copy(parts.at[0], chunk(whole, me), local_sem)
    own.start()
    own.wait()
    for copy in copies:
        copy.wait()
    up_out[...] = adapter_scale * jnp.dot(
        whole[...], cotangent_ref[...], preferred_element_type=jnp.float32
    )
    for copy in later:
        copy.wait()


def return_all(grad_gated_ch, outer_grad_ch, token_t, down_t, whole_cotangent):
    ctx_size, tp_size = lax.axis_size("ctx"), lax.axis_size("tp")
    count = ctx_size * tp_size
    rows, length = grad_gated_ch.shape
    rank = token_t.shape[0]
    tokens = jax.ShapeDtypeStruct((rows * ctx_size, length // ctx_size), jnp.bfloat16)
    dma = pltpu.SemaphoreType.DMA
    return pl.pallas_call(
        functools.partial(return_kernel, ctx_size, tp_size),
        out_shape=(
            tokens,
            tokens,
            jax.ShapeDtypeStruct((rank, rows * ctx_size), jnp.bfloat16),
            jax.ShapeDtypeStruct((rank, whole_cotangent.shape[1]), jnp.float32),
        ),
        in_specs=[pl.BlockSpec(memory_space=pltpu.VMEM)] * 5,
        out_specs=(pl.BlockSpec(memory_space=pltpu.VMEM),) * 4,
        scratch_shapes=[
            pltpu.VMEM((count, 16, 128), jnp.bfloat16),
            pltpu.VMEM((rank, length), jnp.bfloat16),
            dma((count,)),
            dma((count,)),
            dma((count,)),
            dma((count,)),
            dma((3, ctx_size)),
            dma((3, ctx_size)),
            dma,
        ],
        compiler_params=pltpu.CompilerParams(
            collective_id=1, has_side_effects=True, vmem_limit_bytes=40 << 20
        ),
    )(grad_gated_ch, outer_grad_ch, token_t, down_t, whole_cotangent)


exchange_step = 3


def project_kernel(
    ctx_size,
    tp_size,
    cotangent_ref,
    weight_ref,
    up_ref,
    filter_ref,
    gated_ref,
    outer_ref,
    whole_out,
    filter_out,
    gated_out,
    outer_out,
    back_out,
    adapter_out,
    partial,
    landed,
    summed,
    adapter_parts,
    adapter_sum,
    send_relay,
    recv_relay,
    send_part,
    recv_part,
    send_sum,
    recv_sum,
    send_row,
    recv_row,
    send_ad,
    recv_ad,
    send_adsum,
    recv_adsum,
):
    me, count, peer = position()
    ctx, tp = lax.axis_index("ctx"), lax.axis_index("tp")
    width = cotangent_ref.shape[0]
    rows = weight_ref.shape[0] // tp_size
    ch_rows = filter_out.shape[0]
    steps = 2 * (ctx_size - 1) + 1
    greet(count, peer)

    def describe(src, dst, send_sem, recv_sem, device):
        return pltpu.make_async_remote_copy(
            src_ref=src,
            dst_ref=dst,
            send_sem=send_sem,
            recv_sem=recv_sem,
            device_id=device,
            device_id_type=pl.DeviceIdType.MESH,
        )

    def token_rows(block):
        return pl.ds(pl.multiple_of(block * width, 128), width)

    def stage(i):
        hop = (i + 1) // 2
        odd = lax.rem(i, 2)
        block = ctx + hop - 2 * odd * hop
        return hop, 1 - odd, block, jnp.logical_and(block >= 0, block < ctx_size)

    def relay(way, hop, block):
        target = lax.rem(ctx + ctx_size + 1 - 2 * way, ctx_size)
        held = whole_out.at[token_rows(block), :]
        return describe(
            held,
            held,
            send_relay.at[way, hop],
            recv_relay.at[way, hop + 1],
            {"ctx": target, "tp": tp},
        )

    def can_relay(way):
        target = ctx + 1 - 2 * way
        return jnp.logical_and(target >= 0, target < ctx_size)

    whole_out[token_rows(ctx), :] = cotangent_ref[...]
    for way in range(2):
        pl.when(can_relay(way))(lambda way=way: relay(way, 0, ctx).start())

    adapter_parts[0] = lax.dot_general(
        up_ref[...],
        cotangent_ref[...],
        (((1,), (1,)), ((), ())),
        preferred_element_type=jnp.float32,
    ).astype(jnp.bfloat16)
    adapter_copies = []
    for step in range(1, tp_size):
        device = {"ctx": ctx, "tp": lax.rem(tp + step, tp_size)}
        adapter_copies.append(
            push(
                adapter_parts.at[0],
                adapter_parts.at[step],
                send_ad.at[step],
                recv_ad.at[step],
                device,
            )
        )
    for copy in adapter_copies:
        copy.wait()
    adapter_total = adapter_parts[0].astype(jnp.float32)
    for step in range(1, tp_size):
        adapter_total += adapter_parts[step].astype(jnp.float32)
    adapter_sum[...] = adapter_total.astype(jnp.bfloat16)
    adapter_out[:, token_rows(ctx)] = adapter_sum[...]
    later = []
    for step in range(1, ctx_size):
        device = {"ctx": lax.rem(ctx + step, ctx_size), "tp": tp}
        later.append(
            push(
                adapter_sum,
                adapter_out.at[:, token_rows(ctx)],
                send_adsum.at[step],
                recv_adsum.at[step],
                device,
            )
        )

    def exchange(kind, src, dst, step):
        other = lax.rem(ctx + step, ctx_size)
        return describe(
            src.at[pl.ds(pl.multiple_of(other * ch_rows, 16), ch_rows), :],
            dst.at[:, token_rows(ctx)],
            send_row.at[kind, step],
            recv_row.at[kind, step],
            {"ctx": other, "tp": tp},
        )

    pairs = ((filter_ref, filter_out), (gated_ref, gated_out), (outer_ref, outer_out))
    my_rows = pl.ds(pl.multiple_of(ctx * ch_rows, 16), ch_rows)
    for src, dst in pairs:
        dst[:, token_rows(ctx)] = src[my_rows, :]

    def part_copy(block, step):
        other = lax.rem(tp + step, tp_size)
        return describe(
            partial.at[block, step],
            landed.at[block, step],
            send_part.at[block, step],
            recv_part.at[block, step],
            {"ctx": ctx, "tp": other},
        )

    place = ctx * tp_size + tp
    goal_ctx, goal_tp = lax.rem(place, ctx_size), place // ctx_size
    stays = jnp.logical_and(goal_ctx == ctx, goal_tp == tp)

    def sum_copy(block):
        return describe(
            summed.at[block],
            back_out.at[:, token_rows(block)],
            send_sum.at[block],
            recv_sum.at[block],
            {"ctx": goal_ctx, "tp": goal_tp},
        )

    def multiply(block):
        for step in list(range(1, tp_size)) + [0]:
            other = lax.rem(tp + step, tp_size)
            partial[block, step] = lax.dot_general(
                weight_ref[pl.ds(pl.multiple_of(other * rows, 16), rows), :],
                whole_out[token_rows(block), :],
                (((1,), (1,)), ((), ())),
                preferred_element_type=jnp.float32,
            ).astype(jnp.bfloat16)
            if step:
                part_copy(block, step).start()

    def finish(i):
        hop, way, block, valid = stage(i)

        @pl.when(valid)
        def _():
            total = partial[block, 0].astype(jnp.float32)
            for step in range(1, tp_size):
                part_copy(block, step).wait_recv()
                total += landed[block, step].astype(jnp.float32)
            summed[block] = total.astype(jnp.bfloat16)

            @pl.when(stays)
            def _():
                back_out[:, token_rows(block)] = summed[block]

            @pl.when(jnp.logical_not(stays))
            def _():
                sum_copy(block).start()

    def body(i, carry):
        hop, way, block, valid = stage(i)

        @pl.when(valid)
        def _():
            @pl.when(i > 0)
            def _():
                relay(way, hop - 1, block).wait_recv()

                @pl.when(can_relay(way))
                def _():
                    relay(way, hop, block).start()

            multiply(block)

        @pl.when(i == exchange_step)
        def _():
            for kind, (src, dst) in enumerate(pairs):
                for step in range(1, ctx_size):
                    exchange(kind, src, dst, step).start()

        pl.when(i > 0)(lambda: finish(i - 1))
        return carry

    lax.fori_loop(0, steps, body, 0)
    finish(steps - 1)

    for way in range(2):
        for hop in range(ctx_size - 1):
            block = ctx - hop if way == 0 else ctx + hop
            held = jnp.logical_and(block >= 0, block < ctx_size)
            pl.when(jnp.logical_and(held, can_relay(way)))(
                lambda way=way, hop=hop, block=block: relay(way, hop, block).wait_send()
            )
    for block in range(ctx_size):
        for step in range(1, tp_size):
            part_copy(block, step).wait_send()
    for copy in later:
        copy.wait()
    for kind, (src, dst) in enumerate(pairs):
        for step in range(1, ctx_size):
            exchange(kind, src, dst, step).wait()

    @pl.when(jnp.logical_not(stays))
    def _():
        for block in range(ctx_size):
            sum_copy(block).wait()


def project_all(cotangent, weight, up_factor, masked_filter, gated, outer_gate):
    ctx_size, tp_size = lax.axis_size("ctx"), lax.axis_size("tp")
    width, features = cotangent.shape
    length = width * ctx_size
    rows = weight.shape[0] // tp_size
    rank = up_factor.shape[0]
    channels = jax.ShapeDtypeStruct((gated.shape[0] // ctx_size, length), jnp.bfloat16)
    dma = pltpu.SemaphoreType.DMA
    return pl.pallas_call(
        functools.partial(project_kernel, ctx_size, tp_size),
        out_shape=(
            jax.ShapeDtypeStruct((length, features), jnp.bfloat16),
            channels,
            channels,
            channels,
            jax.ShapeDtypeStruct((rows, length), jnp.bfloat16),
            jax.ShapeDtypeStruct((rank, length), jnp.bfloat16),
        ),
        in_specs=[pl.BlockSpec(memory_space=pltpu.VMEM)] * 6,
        out_specs=(pl.BlockSpec(memory_space=pltpu.VMEM),) * 6,
        scratch_shapes=[
            pltpu.VMEM((ctx_size, tp_size, rows, width), jnp.bfloat16),
            pltpu.VMEM((ctx_size, tp_size, rows, width), jnp.bfloat16),
            pltpu.VMEM((ctx_size, rows, width), jnp.bfloat16),
            pltpu.VMEM((tp_size, rank, width), jnp.bfloat16),
            pltpu.VMEM((rank, width), jnp.bfloat16),
            dma((2, ctx_size)),
            dma((2, ctx_size)),
            dma((ctx_size, tp_size)),
            dma((ctx_size, tp_size)),
            dma((ctx_size,)),
            dma((ctx_size,)),
            dma((3, ctx_size)),
            dma((3, ctx_size)),
            dma((tp_size,)),
            dma((tp_size,)),
            dma((ctx_size,)),
            dma((ctx_size,)),
        ],
        compiler_params=pltpu.CompilerParams(
            collective_id=2, has_side_effects=True, vmem_limit_bytes=48 << 20
        ),
    )(cotangent, weight, up_factor, masked_filter, gated, outer_gate)


def token_by_kernel(count, shape, rank):
    return count <= kernel_peers and shape[1] <= dense_length and rank * shape[1] == count * 2048


def local(
    inner_gate_proj,
    outer_gate_proj,
    value_projection,
    channel_filter_lags,
    channel_filter_length,
    output_cotangent,
    output_weight,
    adapter_down_factor,
    adapter_up_factor,
):
    ctx_size, tp_size = lax.axis_size("ctx"), lax.axis_size("tp")
    tok_rows = inner_gate_proj.shape[1]
    lag_index = lax.axis_index("ctx") * tok_rows + lax.broadcasted_iota(
        jnp.int32, channel_filter_lags.shape, 1
    )
    masked_filter = jnp.where(
        lag_index < channel_filter_length[:, None],
        channel_filter_lags,
        jnp.zeros_like(channel_filter_lags),
    ).astype(jnp.bfloat16)
    gated = product_bf(inner_gate_proj, value_projection)
    by_kernel = token_by_kernel(
        ctx_size * tp_size,
        (gated.shape[0] // ctx_size, tok_rows * ctx_size),
        adapter_down_factor.shape[1],
    )
    if by_kernel:
        whole_cotangent, filter_ch, gated_ch, outer_ch, output_backward, adapter_t = project_all(
            output_cotangent,
            output_weight,
            adapter_up_factor,
            masked_filter,
            gated,
            outer_gate_proj,
        )
        output_backward = output_backward.astype(jnp.float32)
        adapter_backward = adapter_t.T
    else:
        whole_cotangent = lax.all_gather(output_cotangent, "ctx", axis=0, tiled=True)
        filter_ch, gated_ch, outer_ch = lax.all_to_all(
            jnp.stack([masked_filter, gated, outer_gate_proj]),
            "ctx",
            split_axis=1,
            concat_axis=2,
            tiled=True,
        )
        partial = lax.dot_general(
            output_weight,
            whole_cotangent,
            (((1,), (1,)), ((), ())),
            preferred_element_type=jnp.float32,
        ).astype(jnp.bfloat16)
        adapter_backward = lax.psum(
            lax.dot_general(
                whole_cotangent,
                adapter_up_factor,
                (((1,), (1,)), ((), ())),
                preferred_element_type=jnp.float32,
            ).astype(jnp.bfloat16),
            "tp",
        )
        scattered = lax.psum_scatter(partial, "tp", scatter_dimension=0, tiled=True)
        moves = [(i, (i % ctx_size) * tp_size + i // ctx_size) for i in range(ctx_size * tp_size)]
        output_backward = lax.ppermute(scattered, ("ctx", "tp"), moves).astype(jnp.float32)
    rows = filter_ch.shape[0]
    down_rows = lax.dynamic_slice_in_dim(
        adapter_down_factor, lax.axis_index("ctx") * rows, rows, axis=0
    )
    adapter_term = lax.dot_general(
        down_rows,
        adapter_backward,
        (((1,), (1,)), ((), ())),
        preferred_element_type=jnp.float32,
    )
    projected_gradient = (output_backward + adapter_term).astype(jnp.bfloat16)
    grad_conv = product_bf(projected_gradient, outer_ch)
    if filter_ch.shape[1] <= dense_length:
        conv_ch, grad_gated_ch = convolve_dense(filter_ch, gated_ch, grad_conv)
    else:
        conv_ch, grad_gated_ch = convolve(filter_ch.astype(jnp.float32), gated_ch, grad_conv)
    block_output = product_bf(outer_ch, conv_ch)
    outer_grad_ch = product_bf(projected_gradient, conv_ch)
    if by_kernel:
        token_t = lax.dot_general(
            down_rows,
            block_output,
            (((0,), (0,)), ((), ())),
            preferred_element_type=jnp.float32,
        ).astype(jnp.bfloat16)
        down_t = lax.dot_general(
            adapter_backward,
            block_output,
            (((0,), (1,)), ((), ())),
            preferred_element_type=jnp.float32,
        ).astype(jnp.bfloat16)
        grad_gated, outer_gate_gradient, down_sum, up_sum = return_all(
            grad_gated_ch, outer_grad_ch, token_t, down_t, whole_cotangent
        )
        return (
            product_bf(grad_gated, value_projection),
            outer_gate_gradient,
            product_bf(grad_gated, inner_gate_proj),
            down_sum.astype(jnp.float32).T * adapter_scale,
            up_sum,
        )
    token_part = lax.dot_general(
        block_output,
        down_rows,
        (((0,), (0,)), ((), ())),
        preferred_element_type=jnp.float32,
    )
    token_adapter = lax.psum(token_part.astype(jnp.bfloat16), ("ctx", "tp"))
    grad_gated, outer_gate_gradient = lax.all_to_all(
        jnp.stack([grad_gated_ch, outer_grad_ch]),
        "ctx",
        split_axis=2,
        concat_axis=1,
        tiled=True,
    )
    down_part = jnp.dot(block_output, adapter_backward, preferred_element_type=jnp.float32)
    down_sum = lax.all_gather(down_part.astype(jnp.bfloat16), "ctx", axis=0, tiled=True)
    up_sum = lax.dot_general(
        token_adapter,
        whole_cotangent,
        (((0,), (0,)), ((), ())),
        preferred_element_type=jnp.float32,
    )
    return (
        product_bf(grad_gated, value_projection),
        outer_gate_gradient,
        product_bf(grad_gated, inner_gate_proj),
        down_sum.astype(jnp.float32) * adapter_scale,
        up_sum * adapter_scale,
    )


def solution(mesh):
    return jax.shard_map(
        local,
        mesh=mesh,
        in_specs=(
            P("tp", ("groups", "ctx")),
            P("tp", ("groups", "ctx")),
            P("tp", ("groups", "ctx")),
            P("tp", "ctx"),
            P("tp"),
            P(("groups", "ctx"), "tp"),
            P("ctx", "tp"),
            P("tp", None),
            P(None, "tp"),
        ),
        out_specs=(
            P("tp", ("groups", "ctx")),
            P("tp", ("groups", "ctx")),
            P("tp", ("groups", "ctx")),
            P(("groups", "tp"), None),
            P("groups", "tp"),
        ),
        check_vma=False,
    )
```

```python
import functools
import math

import jax
import jax.numpy as jnp
import ml_dtypes
import numpy as np
from jax import lax
from jax.experimental import pallas as pl
from jax.experimental.pallas import tpu as pltpu
from jax.sharding import PartitionSpec as P

adapter_scale = 2.0


def product_bf(left, right):
    return (left.astype(jnp.float32) * right.astype(jnp.float32)).astype(jnp.bfloat16)


def dft_table(length):
    across = lax.broadcasted_iota(jnp.int32, (length, length), 0)
    downward = lax.broadcasted_iota(jnp.int32, (length, length), 1)
    angle = -2.0 * math.pi / length * (across * downward % length).astype(jnp.float32)
    return (jnp.cos(angle), jnp.sin(angle))


def twiddle_table(outer, inner):
    total = outer * inner
    first_idx = lax.broadcasted_iota(jnp.int32, (outer, inner), 0)
    second_idx = lax.broadcasted_iota(jnp.int32, (outer, inner), 1)
    angle = -2.0 * math.pi / total * (first_idx * second_idx % total).astype(jnp.float32)
    return (jnp.cos(angle), jnp.sin(angle))


def left_apply(table, field):
    return jnp.einsum("ap,cpq->caq", table, field, precision=lax.Precision.HIGHEST)


def right_apply(field, table):
    return jnp.einsum("caq,qb->cab", field, table, precision=lax.Precision.HIGHEST)


def forward_dft(signal, tables):
    outer_cos, outer_sin, inner_cos, inner_sin, twist_cos, twist_sin = tables
    channels = signal.shape[0]
    block = signal.reshape(channels, outer_cos.shape[0], inner_cos.shape[0])
    first_real = left_apply(outer_cos, block)
    first_imag = left_apply(outer_sin, block)
    turned_real = first_real * twist_cos - first_imag * twist_sin
    turned_imag = first_real * twist_sin + first_imag * twist_cos
    spec_real = right_apply(turned_real, inner_cos) - right_apply(turned_imag, inner_sin)
    spec_imag = right_apply(turned_real, inner_sin) + right_apply(turned_imag, inner_cos)
    return (spec_real, spec_imag)


def inverse_real(spec_real, spec_imag, tables):
    outer_cos, outer_sin, inner_cos, inner_sin, twist_cos, twist_sin = tables
    back_real = right_apply(spec_real, inner_cos) + right_apply(spec_imag, inner_sin)
    back_imag = right_apply(spec_imag, inner_cos) - right_apply(spec_real, inner_sin)
    untwist_real = back_real * twist_cos + back_imag * twist_sin
    untwist_imag = back_imag * twist_cos - back_real * twist_sin
    result = left_apply(outer_cos, untwist_real) + left_apply(outer_sin, untwist_imag)
    total = outer_cos.shape[0] * inner_cos.shape[0]
    return result.reshape(result.shape[0], total) / total


def convolve(taps, gated, grad_conv):
    channels, length = taps.shape
    total = 2 * length
    outer = 1 << (total.bit_length() - 1) // 2
    inner = total // outer
    outer_cos, outer_sin = dft_table(outer)
    inner_cos, inner_sin = dft_table(inner)
    twist_cos, twist_sin = twiddle_table(outer, inner)
    tables = (outer_cos, outer_sin, inner_cos, inner_sin, twist_cos, twist_sin)
    padding = jnp.zeros((channels, length), jnp.float32)

    def spectrum(field):
        return forward_dft(jnp.concatenate([field.astype(jnp.float32), padding], axis=1), tables)

    filt_real, filt_imag = spectrum(taps)
    gated_real, gated_imag = spectrum(gated)
    grad_real, grad_imag = spectrum(grad_conv)
    forward_val = inverse_real(
        filt_real * gated_real - filt_imag * gated_imag,
        filt_real * gated_imag + filt_imag * gated_real,
        tables,
    )[:, :length]
    backward_val = inverse_real(
        filt_real * grad_real + filt_imag * grad_imag,
        filt_real * grad_imag - filt_imag * grad_real,
        tables,
    )[:, :length]
    return (forward_val.astype(jnp.bfloat16), backward_val.astype(jnp.bfloat16))


dense_length = 2048


def dense_table(length):
    lag = np.arange(length, dtype=np.int64)[:, None]
    freq = np.arange(length, dtype=np.int64)[None, :]
    angle = np.pi / (2 * length) * (lag * (2 * freq + 1) % (4 * length))
    table = np.concatenate([np.cos(angle), np.sin(angle)], axis=1)
    return jnp.asarray(table.astype(ml_dtypes.bfloat16))


def dense_spectrum(field, table):
    spec = jnp.dot(field, table, preferred_element_type=jnp.float32)
    return spec[:, : field.shape[1]], spec[:, field.shape[1] :]


def dense_inverse(cos_part, sin_part, table):
    spec = jnp.concatenate([cos_part, sin_part], axis=1).astype(jnp.bfloat16)
    field = lax.dot_general(
        spec, table, (((1,), (1,)), ((), ())), preferred_element_type=jnp.float32
    )
    return (field * (1.0 / table.shape[0])).astype(jnp.bfloat16)


def convolve_dense(taps, gated, grad_conv):
    table = dense_table(taps.shape[1])
    filt_cos, filt_sin = dense_spectrum(taps, table)
    gated_cos, gated_sin = dense_spectrum(gated, table)
    conv = dense_inverse(
        filt_cos * gated_cos - filt_sin * gated_sin,
        filt_cos * gated_sin + filt_sin * gated_cos,
        table,
    )
    grad_cos, grad_sin = dense_spectrum(grad_conv, table)
    back = dense_inverse(
        filt_cos * grad_cos + filt_sin * grad_sin,
        filt_cos * grad_sin - filt_sin * grad_cos,
        table,
    )
    return conv, back


kernel_peers = 16


def position():
    ctx_size, tp_size = lax.axis_size("ctx"), lax.axis_size("tp")
    count = ctx_size * tp_size
    me = lax.axis_index("ctx") * tp_size + lax.axis_index("tp")

    def peer(step):
        other = lax.rem(me + step, count)
        return {"ctx": other // tp_size, "tp": lax.rem(other, tp_size)}

    return me, count, peer


def greet(count, peer):
    barrier = pltpu.get_barrier_semaphore()
    for step in range(1, count):
        pl.semaphore_signal(
            barrier, inc=1, device_id=peer(step), device_id_type=pl.DeviceIdType.MESH
        )
    pl.semaphore_wait(barrier, count - 1)


def push(src, dst, send_sem, recv_sem, device):
    copy = pltpu.make_async_remote_copy(
        src_ref=src,
        dst_ref=dst,
        send_sem=send_sem,
        recv_sem=recv_sem,
        device_id=device,
        device_id_type=pl.DeviceIdType.MESH,
    )
    copy.start()
    return copy


def return_kernel(
    ctx_size,
    tp_size,
    grad_ref,
    outer_ref,
    token_ref,
    down_ref,
    cotangent_ref,
    grad_out,
    outer_out,
    down_out,
    up_out,
    parts,
    whole,
    send_tok,
    recv_tok,
    send_all,
    recv_all,
    send_row,
    recv_row,
    local_sem,
):
    me, count, peer = position()
    ctx, tp = lax.axis_index("ctx"), lax.axis_index("tp")
    rows, length = grad_ref.shape
    width = length // ctx_size
    lanes = length // 128
    greet(count, peer)

    def chunk(ref, place):
        top = pl.multiple_of(place // lanes * 16, 16)
        left = pl.multiple_of(lax.rem(place, lanes) * 128, 128)
        return ref.at[pl.ds(top, 16), pl.ds(left, 128)]

    copies = []
    for step in range(1, count):
        copies.append(
            push(
                chunk(token_ref, lax.rem(me + step, count)),
                parts.at[step],
                send_tok.at[step],
                recv_tok.at[step],
                peer(step),
            )
        )
    my_rows = pl.ds(pl.multiple_of(ctx * rows, 16), rows)
    my_cols = pl.ds(pl.multiple_of(ctx * width, 128), width)
    my_lags = pl.ds(pl.multiple_of(ctx * rows, 128), rows)
    later = []
    for step in range(1, ctx_size):
        other = lax.rem(ctx + step, ctx_size)
        device = {"ctx": other, "tp": tp}
        cols = pl.ds(pl.multiple_of(other * width, 128), width)
        moves = (
            (down_ref, down_out.at[:, my_lags]),
            (grad_ref.at[:, cols], grad_out.at[my_rows, :]),
            (outer_ref.at[:, cols], outer_out.at[my_rows, :]),
        )
        for kind, (src, dst) in enumerate(moves):
            later.append(push(src, dst, send_row.at[kind, step], recv_row.at[kind, step], device))
    down_out[:, my_lags] = down_ref[...]
    grad_out[my_rows, :] = grad_ref[:, my_cols]
    outer_out[my_rows, :] = outer_ref[:, my_cols]

    own = pltpu.make_async_copy(chunk(token_ref, me), parts.at[0], local_sem)
    own.start()
    own.wait()
    total = parts[0].astype(jnp.float32)
    for step in range(1, count):
        copies[step - 1].wait_recv()
        total += parts[step].astype(jnp.float32)
    for copy in copies:
        copy.wait_send()
    parts[0] = total.astype(jnp.bfloat16)
    copies = []
    for step in range(1, count):
        copies.append(
            push(
                parts.at[0],
                chunk(whole, me),
                send_all.at[step],
                recv_all.at[step],
                peer(step),
            )
        )
    own = pltpu.make_async_copy(parts.at[0], chunk(whole, me), local_sem)
    own.start()
    own.wait()
    for copy in copies:
        copy.wait()
    up_out[...] = adapter_scale * jnp.dot(
        whole[...], cotangent_ref[...], preferred_element_type=jnp.float32
    )
    for copy in later:
        copy.wait()


def return_all(grad_gated_ch, outer_grad_ch, token_t, down_t, whole_cotangent):
    ctx_size, tp_size = lax.axis_size("ctx"), lax.axis_size("tp")
    count = ctx_size * tp_size
    rows, length = grad_gated_ch.shape
    rank = token_t.shape[0]
    tokens = jax.ShapeDtypeStruct((rows * ctx_size, length // ctx_size), jnp.bfloat16)
    dma = pltpu.SemaphoreType.DMA
    return pl.pallas_call(
        functools.partial(return_kernel, ctx_size, tp_size),
        out_shape=(
            tokens,
            tokens,
            jax.ShapeDtypeStruct((rank, rows * ctx_size), jnp.bfloat16),
            jax.ShapeDtypeStruct((rank, whole_cotangent.shape[1]), jnp.float32),
        ),
        in_specs=[pl.BlockSpec(memory_space=pltpu.VMEM)] * 5,
        out_specs=(pl.BlockSpec(memory_space=pltpu.VMEM),) * 4,
        scratch_shapes=[
            pltpu.VMEM((count, 16, 128), jnp.bfloat16),
            pltpu.VMEM((rank, length), jnp.bfloat16),
            dma((count,)),
            dma((count,)),
            dma((count,)),
            dma((count,)),
            dma((3, ctx_size)),
            dma((3, ctx_size)),
            dma,
        ],
        compiler_params=pltpu.CompilerParams(
            collective_id=1, has_side_effects=True, vmem_limit_bytes=40 << 20
        ),
    )(grad_gated_ch, outer_grad_ch, token_t, down_t, whole_cotangent)


exchange_step = 4


def project_kernel(
    ctx_size,
    tp_size,
    cotangent_ref,
    weight_ref,
    up_ref,
    filter_ref,
    gated_ref,
    outer_ref,
    whole_out,
    filter_out,
    gated_out,
    outer_out,
    back_out,
    adapter_out,
    partial,
    landed,
    summed,
    adapter_parts,
    adapter_sum,
    send_relay,
    recv_relay,
    send_part,
    recv_part,
    send_sum,
    recv_sum,
    send_row,
    recv_row,
    send_ad,
    recv_ad,
    send_adsum,
    recv_adsum,
):
    me, count, peer = position()
    ctx, tp = lax.axis_index("ctx"), lax.axis_index("tp")
    width = cotangent_ref.shape[0]
    rows = weight_ref.shape[0] // tp_size
    ch_rows = filter_out.shape[0]
    steps = 2 * (ctx_size - 1) + 1
    greet(count, peer)

    def describe(src, dst, send_sem, recv_sem, device):
        return pltpu.make_async_remote_copy(
            src_ref=src,
            dst_ref=dst,
            send_sem=send_sem,
            recv_sem=recv_sem,
            device_id=device,
            device_id_type=pl.DeviceIdType.MESH,
        )

    def token_rows(block):
        return pl.ds(pl.multiple_of(block * width, 128), width)

    def stage(i):
        hop = (i + 1) // 2
        odd = lax.rem(i, 2)
        block = ctx + hop - 2 * odd * hop
        return hop, 1 - odd, block, jnp.logical_and(block >= 0, block < ctx_size)

    def relay(way, hop, block, half):
        target = lax.rem(ctx + ctx_size + 1 - 2 * way, ctx_size)
        top = pl.multiple_of(block * width + half * (width // 2), 16)
        held = whole_out.at[pl.ds(top, width // 2), :]
        return describe(
            held,
            held,
            send_relay.at[2 * way + half, hop],
            recv_relay.at[2 * way + half, hop + 1],
            {"ctx": target, "tp": tp},
        )

    def can_relay(way):
        target = ctx + 1 - 2 * way
        return jnp.logical_and(target >= 0, target < ctx_size)

    whole_out[token_rows(ctx), :] = cotangent_ref[...]
    for half in range(2):
        for way in range(2):
            pl.when(can_relay(way))(lambda way=way, half=half: relay(way, 0, ctx, half).start())

    adapter_parts[0] = lax.dot_general(
        up_ref[...],
        cotangent_ref[...],
        (((1,), (1,)), ((), ())),
        preferred_element_type=jnp.float32,
    ).astype(jnp.bfloat16)
    adapter_copies = []
    for step in range(1, tp_size):
        device = {"ctx": ctx, "tp": lax.rem(tp + step, tp_size)}
        adapter_copies.append(
            push(
                adapter_parts.at[0],
                adapter_parts.at[step],
                send_ad.at[step],
                recv_ad.at[step],
                device,
            )
        )
    for copy in adapter_copies:
        copy.wait()
    adapter_total = adapter_parts[0].astype(jnp.float32)
    for step in range(1, tp_size):
        adapter_total += adapter_parts[step].astype(jnp.float32)
    adapter_sum[...] = adapter_total.astype(jnp.bfloat16)
    adapter_out[:, token_rows(ctx)] = adapter_sum[...]
    later = []
    for step in range(1, ctx_size):
        device = {"ctx": lax.rem(ctx + step, ctx_size), "tp": tp}
        later.append(
            push(
                adapter_sum,
                adapter_out.at[:, token_rows(ctx)],
                send_adsum.at[step],
                recv_adsum.at[step],
                device,
            )
        )

    def exchange(kind, src, dst, step):
        other = lax.rem(ctx + step, ctx_size)
        return describe(
            src.at[pl.ds(pl.multiple_of(other * ch_rows, 16), ch_rows), :],
            dst.at[:, token_rows(ctx)],
            send_row.at[kind, step],
            recv_row.at[kind, step],
            {"ctx": other, "tp": tp},
        )

    pairs = ((filter_ref, filter_out), (gated_ref, gated_out), (outer_ref, outer_out))
    my_rows = pl.ds(pl.multiple_of(ctx * ch_rows, 16), ch_rows)
    for src, dst in pairs:
        dst[:, token_rows(ctx)] = src[my_rows, :]

    def part_copy(block, step):
        other = lax.rem(tp + step, tp_size)
        return describe(
            partial.at[block, step],
            landed.at[block, step],
            send_part.at[block, step],
            recv_part.at[block, step],
            {"ctx": ctx, "tp": other},
        )

    place = ctx * tp_size + tp
    goal_ctx, goal_tp = lax.rem(place, ctx_size), place // ctx_size
    stays = jnp.logical_and(goal_ctx == ctx, goal_tp == tp)

    def sum_copy(block):
        return describe(
            summed.at[block],
            back_out.at[:, token_rows(block)],
            send_sum.at[block],
            recv_sum.at[block],
            {"ctx": goal_ctx, "tp": goal_tp},
        )

    def multiply(block):
        for step in list(range(1, tp_size)) + [0]:
            other = lax.rem(tp + step, tp_size)
            partial[block, step] = lax.dot_general(
                weight_ref[pl.ds(pl.multiple_of(other * rows, 16), rows), :],
                whole_out[token_rows(block), :],
                (((1,), (1,)), ((), ())),
                preferred_element_type=jnp.float32,
            ).astype(jnp.bfloat16)
            if step:
                part_copy(block, step).start()

    def finish(i):
        hop, way, block, valid = stage(i)

        @pl.when(valid)
        def _():
            total = partial[block, 0].astype(jnp.float32)
            for step in range(1, tp_size):
                part_copy(block, step).wait_recv()
                total += landed[block, step].astype(jnp.float32)
            summed[block] = total.astype(jnp.bfloat16)

            @pl.when(stays)
            def _():
                back_out[:, token_rows(block)] = summed[block]

            @pl.when(jnp.logical_not(stays))
            def _():
                sum_copy(block).start()

    def pass_on(side, hop, half):
        block = ctx - hop if side == 0 else ctx + hop

        @pl.when(jnp.logical_and(block >= 0, block < ctx_size))
        def _():
            relay(side, hop - 1, block, half).wait_recv()

            @pl.when(can_relay(side))
            def _():
                relay(side, hop, block, half).start()

    def body(i, carry):
        hop, way, block, valid = stage(i)

        @pl.when(way == 0)
        def _():
            for half in range(2):
                for side in range(2):
                    pass_on(side, hop, half)

        pl.when(valid)(lambda: multiply(block))

        @pl.when(i == exchange_step)
        def _():
            for kind, (src, dst) in enumerate(pairs):
                for step in range(1, ctx_size):
                    exchange(kind, src, dst, step).start()

        pl.when(i > 0)(lambda: finish(i - 1))
        return carry

    lax.fori_loop(0, steps, body, 0)
    finish(steps - 1)

    for way in range(2):
        for hop in range(ctx_size - 1):
            block = ctx - hop if way == 0 else ctx + hop
            held = jnp.logical_and(block >= 0, block < ctx_size)
            for half in range(2):
                pl.when(jnp.logical_and(held, can_relay(way)))(
                    lambda way=way, hop=hop, block=block, half=half: relay(
                        way, hop, block, half
                    ).wait_send()
                )
    for block in range(ctx_size):
        for step in range(1, tp_size):
            part_copy(block, step).wait_send()
    for copy in later:
        copy.wait()
    for kind, (src, dst) in enumerate(pairs):
        for step in range(1, ctx_size):
            exchange(kind, src, dst, step).wait()

    @pl.when(jnp.logical_not(stays))
    def _():
        for block in range(ctx_size):
            sum_copy(block).wait()


def project_all(cotangent, weight, up_factor, masked_filter, gated, outer_gate):
    ctx_size, tp_size = lax.axis_size("ctx"), lax.axis_size("tp")
    width, features = cotangent.shape
    length = width * ctx_size
    rows = weight.shape[0] // tp_size
    rank = up_factor.shape[0]
    channels = jax.ShapeDtypeStruct((gated.shape[0] // ctx_size, length), jnp.bfloat16)
    dma = pltpu.SemaphoreType.DMA
    return pl.pallas_call(
        functools.partial(project_kernel, ctx_size, tp_size),
        out_shape=(
            jax.ShapeDtypeStruct((length, features), jnp.bfloat16),
            channels,
            channels,
            channels,
            jax.ShapeDtypeStruct((rows, length), jnp.bfloat16),
            jax.ShapeDtypeStruct((rank, length), jnp.bfloat16),
        ),
        in_specs=[pl.BlockSpec(memory_space=pltpu.VMEM)] * 6,
        out_specs=(pl.BlockSpec(memory_space=pltpu.VMEM),) * 6,
        scratch_shapes=[
            pltpu.VMEM((ctx_size, tp_size, rows, width), jnp.bfloat16),
            pltpu.VMEM((ctx_size, tp_size, rows, width), jnp.bfloat16),
            pltpu.VMEM((ctx_size, rows, width), jnp.bfloat16),
            pltpu.VMEM((tp_size, rank, width), jnp.bfloat16),
            pltpu.VMEM((rank, width), jnp.bfloat16),
            dma((4, ctx_size)),
            dma((4, ctx_size)),
            dma((ctx_size, tp_size)),
            dma((ctx_size, tp_size)),
            dma((ctx_size,)),
            dma((ctx_size,)),
            dma((3, ctx_size)),
            dma((3, ctx_size)),
            dma((tp_size,)),
            dma((tp_size,)),
            dma((ctx_size,)),
            dma((ctx_size,)),
        ],
        compiler_params=pltpu.CompilerParams(
            collective_id=2, has_side_effects=True, vmem_limit_bytes=48 << 20
        ),
    )(cotangent, weight, up_factor, masked_filter, gated, outer_gate)


def token_by_kernel(count, shape, rank):
    return count <= kernel_peers and shape[1] <= dense_length and rank * shape[1] == count * 2048


def local(
    inner_gate_proj,
    outer_gate_proj,
    value_projection,
    channel_filter_lags,
    channel_filter_length,
    output_cotangent,
    output_weight,
    adapter_down_factor,
    adapter_up_factor,
):
    ctx_size, tp_size = lax.axis_size("ctx"), lax.axis_size("tp")
    tok_rows = inner_gate_proj.shape[1]
    lag_index = lax.axis_index("ctx") * tok_rows + lax.broadcasted_iota(
        jnp.int32, channel_filter_lags.shape, 1
    )
    masked_filter = jnp.where(
        lag_index < channel_filter_length[:, None],
        channel_filter_lags,
        jnp.zeros_like(channel_filter_lags),
    ).astype(jnp.bfloat16)
    gated = product_bf(inner_gate_proj, value_projection)
    by_kernel = token_by_kernel(
        ctx_size * tp_size,
        (gated.shape[0] // ctx_size, tok_rows * ctx_size),
        adapter_down_factor.shape[1],
    )
    if by_kernel:
        whole_cotangent, filter_ch, gated_ch, outer_ch, output_backward, adapter_t = project_all(
            output_cotangent,
            output_weight,
            adapter_up_factor,
            masked_filter,
            gated,
            outer_gate_proj,
        )
        output_backward = output_backward.astype(jnp.float32)
        adapter_backward = adapter_t.T
    else:
        whole_cotangent = lax.all_gather(output_cotangent, "ctx", axis=0, tiled=True)
        filter_ch, gated_ch, outer_ch = lax.all_to_all(
            jnp.stack([masked_filter, gated, outer_gate_proj]),
            "ctx",
            split_axis=1,
            concat_axis=2,
            tiled=True,
        )
        partial = lax.dot_general(
            output_weight,
            whole_cotangent,
            (((1,), (1,)), ((), ())),
            preferred_element_type=jnp.float32,
        ).astype(jnp.bfloat16)
        adapter_backward = lax.psum(
            lax.dot_general(
                whole_cotangent,
                adapter_up_factor,
                (((1,), (1,)), ((), ())),
                preferred_element_type=jnp.float32,
            ).astype(jnp.bfloat16),
            "tp",
        )
        scattered = lax.psum_scatter(partial, "tp", scatter_dimension=0, tiled=True)
        moves = [(i, (i % ctx_size) * tp_size + i // ctx_size) for i in range(ctx_size * tp_size)]
        output_backward = lax.ppermute(scattered, ("ctx", "tp"), moves).astype(jnp.float32)
    rows = filter_ch.shape[0]
    down_rows = lax.dynamic_slice_in_dim(
        adapter_down_factor, lax.axis_index("ctx") * rows, rows, axis=0
    )
    adapter_term = lax.dot_general(
        down_rows,
        adapter_backward,
        (((1,), (1,)), ((), ())),
        preferred_element_type=jnp.float32,
    )
    projected_gradient = (output_backward + adapter_term).astype(jnp.bfloat16)
    grad_conv = product_bf(projected_gradient, outer_ch)
    if filter_ch.shape[1] <= dense_length:
        conv_ch, grad_gated_ch = convolve_dense(filter_ch, gated_ch, grad_conv)
    else:
        conv_ch, grad_gated_ch = convolve(filter_ch.astype(jnp.float32), gated_ch, grad_conv)
    block_output = product_bf(outer_ch, conv_ch)
    outer_grad_ch = product_bf(projected_gradient, conv_ch)
    if by_kernel:
        token_t = lax.dot_general(
            down_rows,
            block_output,
            (((0,), (0,)), ((), ())),
            preferred_element_type=jnp.float32,
        ).astype(jnp.bfloat16)
        down_t = lax.dot_general(
            adapter_backward,
            block_output,
            (((0,), (1,)), ((), ())),
            preferred_element_type=jnp.float32,
        ).astype(jnp.bfloat16)
        grad_gated, outer_gate_gradient, down_sum, up_sum = return_all(
            grad_gated_ch, outer_grad_ch, token_t, down_t, whole_cotangent
        )
        return (
            product_bf(grad_gated, value_projection),
            outer_gate_gradient,
            product_bf(grad_gated, inner_gate_proj),
            down_sum.astype(jnp.float32).T * adapter_scale,
            up_sum,
        )
    token_part = lax.dot_general(
        block_output,
        down_rows,
        (((0,), (0,)), ((), ())),
        preferred_element_type=jnp.float32,
    )
    token_adapter = lax.psum(token_part.astype(jnp.bfloat16), ("ctx", "tp"))
    grad_gated, outer_gate_gradient = lax.all_to_all(
        jnp.stack([grad_gated_ch, outer_grad_ch]),
        "ctx",
        split_axis=2,
        concat_axis=1,
        tiled=True,
    )
    down_part = jnp.dot(block_output, adapter_backward, preferred_element_type=jnp.float32)
    down_sum = lax.all_gather(down_part.astype(jnp.bfloat16), "ctx", axis=0, tiled=True)
    up_sum = lax.dot_general(
        token_adapter,
        whole_cotangent,
        (((0,), (0,)), ((), ())),
        preferred_element_type=jnp.float32,
    )
    return (
        product_bf(grad_gated, value_projection),
        outer_gate_gradient,
        product_bf(grad_gated, inner_gate_proj),
        down_sum.astype(jnp.float32) * adapter_scale,
        up_sum * adapter_scale,
    )


def solution(mesh):
    return jax.shard_map(
        local,
        mesh=mesh,
        in_specs=(
            P("tp", ("groups", "ctx")),
            P("tp", ("groups", "ctx")),
            P("tp", ("groups", "ctx")),
            P("tp", "ctx"),
            P("tp"),
            P(("groups", "ctx"), "tp"),
            P("ctx", "tp"),
            P("tp", None),
            P(None, "tp"),
        ),
        out_specs=(
            P("tp", ("groups", "ctx")),
            P("tp", ("groups", "ctx")),
            P("tp", ("groups", "ctx")),
            P(("groups", "tp"), None),
            P("groups", "tp"),
        ),
        check_vma=False,
    )
```

```python
import functools
import math

import jax
import jax.numpy as jnp
import ml_dtypes
import numpy as np
from jax import lax
from jax.experimental import pallas as pl
from jax.experimental.pallas import tpu as pltpu
from jax.sharding import PartitionSpec as P

adapter_scale = 2.0


def product_bf(left, right):
    return (left.astype(jnp.float32) * right.astype(jnp.float32)).astype(jnp.bfloat16)


def dft_table(length):
    across = lax.broadcasted_iota(jnp.int32, (length, length), 0)
    downward = lax.broadcasted_iota(jnp.int32, (length, length), 1)
    angle = -2.0 * math.pi / length * (across * downward % length).astype(jnp.float32)
    return (jnp.cos(angle), jnp.sin(angle))


def twiddle_table(outer, inner):
    total = outer * inner
    first_idx = lax.broadcasted_iota(jnp.int32, (outer, inner), 0)
    second_idx = lax.broadcasted_iota(jnp.int32, (outer, inner), 1)
    angle = -2.0 * math.pi / total * (first_idx * second_idx % total).astype(jnp.float32)
    return (jnp.cos(angle), jnp.sin(angle))


def left_apply(table, field):
    return jnp.einsum("ap,cpq->caq", table, field, precision=lax.Precision.HIGHEST)


def right_apply(field, table):
    return jnp.einsum("caq,qb->cab", field, table, precision=lax.Precision.HIGHEST)


def forward_dft(signal, tables):
    outer_cos, outer_sin, inner_cos, inner_sin, twist_cos, twist_sin = tables
    channels = signal.shape[0]
    block = signal.reshape(channels, outer_cos.shape[0], inner_cos.shape[0])
    first_real = left_apply(outer_cos, block)
    first_imag = left_apply(outer_sin, block)
    turned_real = first_real * twist_cos - first_imag * twist_sin
    turned_imag = first_real * twist_sin + first_imag * twist_cos
    spec_real = right_apply(turned_real, inner_cos) - right_apply(turned_imag, inner_sin)
    spec_imag = right_apply(turned_real, inner_sin) + right_apply(turned_imag, inner_cos)
    return (spec_real, spec_imag)


def inverse_real(spec_real, spec_imag, tables):
    outer_cos, outer_sin, inner_cos, inner_sin, twist_cos, twist_sin = tables
    back_real = right_apply(spec_real, inner_cos) + right_apply(spec_imag, inner_sin)
    back_imag = right_apply(spec_imag, inner_cos) - right_apply(spec_real, inner_sin)
    untwist_real = back_real * twist_cos + back_imag * twist_sin
    untwist_imag = back_imag * twist_cos - back_real * twist_sin
    result = left_apply(outer_cos, untwist_real) + left_apply(outer_sin, untwist_imag)
    total = outer_cos.shape[0] * inner_cos.shape[0]
    return result.reshape(result.shape[0], total) / total


def convolve(taps, gated, grad_conv):
    channels, length = taps.shape
    total = 2 * length
    outer = 1 << (total.bit_length() - 1) // 2
    inner = total // outer
    outer_cos, outer_sin = dft_table(outer)
    inner_cos, inner_sin = dft_table(inner)
    twist_cos, twist_sin = twiddle_table(outer, inner)
    tables = (outer_cos, outer_sin, inner_cos, inner_sin, twist_cos, twist_sin)
    padding = jnp.zeros((channels, length), jnp.float32)

    def spectrum(field):
        return forward_dft(jnp.concatenate([field.astype(jnp.float32), padding], axis=1), tables)

    filt_real, filt_imag = spectrum(taps)
    gated_real, gated_imag = spectrum(gated)
    grad_real, grad_imag = spectrum(grad_conv)
    forward_val = inverse_real(
        filt_real * gated_real - filt_imag * gated_imag,
        filt_real * gated_imag + filt_imag * gated_real,
        tables,
    )[:, :length]
    backward_val = inverse_real(
        filt_real * grad_real + filt_imag * grad_imag,
        filt_real * grad_imag - filt_imag * grad_real,
        tables,
    )[:, :length]
    return (forward_val.astype(jnp.bfloat16), backward_val.astype(jnp.bfloat16))


dense_length = 2048


def dense_table(length):
    lag = np.arange(length, dtype=np.int64)[:, None]
    freq = np.arange(length, dtype=np.int64)[None, :]
    angle = np.pi / (2 * length) * (lag * (2 * freq + 1) % (4 * length))
    table = np.concatenate([np.cos(angle), np.sin(angle)], axis=1)
    return jnp.asarray(table.astype(ml_dtypes.bfloat16))


def dense_spectrum(field, table):
    spec = jnp.dot(field, table, preferred_element_type=jnp.float32)
    return spec[:, : field.shape[1]], spec[:, field.shape[1] :]


def dense_inverse(cos_part, sin_part, table):
    spec = jnp.concatenate([cos_part, sin_part], axis=1).astype(jnp.bfloat16)
    field = lax.dot_general(
        spec, table, (((1,), (1,)), ((), ())), preferred_element_type=jnp.float32
    )
    return (field * (1.0 / table.shape[0])).astype(jnp.bfloat16)


def convolve_dense(taps, gated, grad_conv):
    table = dense_table(taps.shape[1])
    filt_cos, filt_sin = dense_spectrum(taps, table)
    gated_cos, gated_sin = dense_spectrum(gated, table)
    conv = dense_inverse(
        filt_cos * gated_cos - filt_sin * gated_sin,
        filt_cos * gated_sin + filt_sin * gated_cos,
        table,
    )
    grad_cos, grad_sin = dense_spectrum(grad_conv, table)
    back = dense_inverse(
        filt_cos * grad_cos + filt_sin * grad_sin,
        filt_cos * grad_sin - filt_sin * grad_cos,
        table,
    )
    return conv, back


kernel_peers = 16


def position():
    ctx_size, tp_size = lax.axis_size("ctx"), lax.axis_size("tp")
    count = ctx_size * tp_size
    me = lax.axis_index("ctx") * tp_size + lax.axis_index("tp")

    def peer(step):
        other = lax.rem(me + step, count)
        return {"ctx": other // tp_size, "tp": lax.rem(other, tp_size)}

    return me, count, peer


def greet(count, peer):
    barrier = pltpu.get_barrier_semaphore()
    for step in range(1, count):
        pl.semaphore_signal(
            barrier, inc=1, device_id=peer(step), device_id_type=pl.DeviceIdType.MESH
        )
    pl.semaphore_wait(barrier, count - 1)


def push(src, dst, send_sem, recv_sem, device):
    copy = pltpu.make_async_remote_copy(
        src_ref=src,
        dst_ref=dst,
        send_sem=send_sem,
        recv_sem=recv_sem,
        device_id=device,
        device_id_type=pl.DeviceIdType.MESH,
    )
    copy.start()
    return copy


def return_kernel(
    ctx_size,
    tp_size,
    grad_ref,
    outer_ref,
    token_ref,
    down_ref,
    cotangent_any,
    grad_out,
    outer_out,
    down_out,
    up_out,
    parts,
    whole,
    send_tok,
    recv_tok,
    send_all,
    recv_all,
    send_row,
    recv_row,
    local_sem,
    cotangent_ref,
    load_sem,
):
    load = pltpu.make_async_copy(cotangent_any, cotangent_ref, load_sem)
    load.start()
    me, count, peer = position()
    ctx, tp = lax.axis_index("ctx"), lax.axis_index("tp")
    rows, length = grad_ref.shape
    width = length // ctx_size
    lanes = length // 128
    greet(count, peer)

    def chunk(ref, place):
        top = pl.multiple_of(place // lanes * 16, 16)
        left = pl.multiple_of(lax.rem(place, lanes) * 128, 128)
        return ref.at[pl.ds(top, 16), pl.ds(left, 128)]

    copies = []
    for step in range(1, count):
        copies.append(
            push(
                chunk(token_ref, lax.rem(me + step, count)),
                parts.at[step],
                send_tok.at[step],
                recv_tok.at[step],
                peer(step),
            )
        )
    my_rows = pl.ds(pl.multiple_of(ctx * rows, 16), rows)
    my_cols = pl.ds(pl.multiple_of(ctx * width, 128), width)
    my_lags = pl.ds(pl.multiple_of(ctx * rows, 128), rows)
    later = []
    for step in range(1, ctx_size):
        other = lax.rem(ctx + step, ctx_size)
        device = {"ctx": other, "tp": tp}
        cols = pl.ds(pl.multiple_of(other * width, 128), width)
        moves = (
            (down_ref, down_out.at[:, my_lags]),
            (grad_ref.at[:, cols], grad_out.at[my_rows, :]),
            (outer_ref.at[:, cols], outer_out.at[my_rows, :]),
        )
        for kind, (src, dst) in enumerate(moves):
            later.append(push(src, dst, send_row.at[kind, step], recv_row.at[kind, step], device))
    down_out[:, my_lags] = down_ref[...]
    grad_out[my_rows, :] = grad_ref[:, my_cols]
    outer_out[my_rows, :] = outer_ref[:, my_cols]

    own = pltpu.make_async_copy(chunk(token_ref, me), parts.at[0], local_sem)
    own.start()
    own.wait()
    total = parts[0].astype(jnp.float32)
    for step in range(1, count):
        copies[step - 1].wait_recv()
        total += parts[step].astype(jnp.float32)
    for copy in copies:
        copy.wait_send()
    parts[0] = total.astype(jnp.bfloat16)
    copies = []
    for step in range(1, count):
        copies.append(
            push(
                parts.at[0],
                chunk(whole, me),
                send_all.at[step],
                recv_all.at[step],
                peer(step),
            )
        )
    own = pltpu.make_async_copy(parts.at[0], chunk(whole, me), local_sem)
    own.start()
    own.wait()
    for copy in copies:
        copy.wait()
    load.wait()
    up_out[...] = adapter_scale * jnp.dot(
        whole[...], cotangent_ref[...], preferred_element_type=jnp.float32
    )
    for copy in later:
        copy.wait()


def return_all(grad_gated_ch, outer_grad_ch, token_t, down_t, whole_cotangent):
    ctx_size, tp_size = lax.axis_size("ctx"), lax.axis_size("tp")
    count = ctx_size * tp_size
    rows, length = grad_gated_ch.shape
    rank = token_t.shape[0]
    tokens = jax.ShapeDtypeStruct((rows * ctx_size, length // ctx_size), jnp.bfloat16)
    dma = pltpu.SemaphoreType.DMA
    return pl.pallas_call(
        functools.partial(return_kernel, ctx_size, tp_size),
        out_shape=(
            tokens,
            tokens,
            jax.ShapeDtypeStruct((rank, rows * ctx_size), jnp.bfloat16),
            jax.ShapeDtypeStruct((rank, whole_cotangent.shape[1]), jnp.float32),
        ),
        in_specs=[pl.BlockSpec(memory_space=pltpu.VMEM)] * 4
        + [pl.BlockSpec(memory_space=pl.ANY)],
        out_specs=(pl.BlockSpec(memory_space=pltpu.VMEM),) * 4,
        scratch_shapes=[
            pltpu.VMEM((count, 16, 128), jnp.bfloat16),
            pltpu.VMEM((rank, length), jnp.bfloat16),
            dma((count,)),
            dma((count,)),
            dma((count,)),
            dma((count,)),
            dma((3, ctx_size)),
            dma((3, ctx_size)),
            dma,
            pltpu.VMEM(whole_cotangent.shape, jnp.bfloat16),
            dma,
        ],
        compiler_params=pltpu.CompilerParams(
            collective_id=1, has_side_effects=True, vmem_limit_bytes=40 << 20
        ),
    )(grad_gated_ch, outer_grad_ch, token_t, down_t, whole_cotangent)


exchange_step = 4


def project_kernel(
    ctx_size,
    tp_size,
    cotangent_ref,
    weight_any,
    up_ref,
    filter_ref,
    gated_ref,
    outer_ref,
    whole_any,
    filter_out,
    gated_out,
    outer_out,
    back_out,
    adapter_out,
    partial,
    landed,
    summed,
    adapter_parts,
    adapter_sum,
    send_relay,
    recv_relay,
    send_part,
    recv_part,
    send_sum,
    recv_sum,
    send_row,
    recv_row,
    send_ad,
    recv_ad,
    send_adsum,
    recv_adsum,
    weight_ref,
    whole_out,
    load_sem,
    store_sem,
):
    load = pltpu.make_async_copy(weight_any, weight_ref, load_sem)
    load.start()
    me, count, peer = position()
    ctx, tp = lax.axis_index("ctx"), lax.axis_index("tp")
    width = cotangent_ref.shape[0]
    rows = weight_ref.shape[0] // tp_size
    ch_rows = filter_out.shape[0]
    steps = 2 * (ctx_size - 1) + 1
    greet(count, peer)

    def describe(src, dst, send_sem, recv_sem, device):
        return pltpu.make_async_remote_copy(
            src_ref=src,
            dst_ref=dst,
            send_sem=send_sem,
            recv_sem=recv_sem,
            device_id=device,
            device_id_type=pl.DeviceIdType.MESH,
        )

    def token_rows(block):
        return pl.ds(pl.multiple_of(block * width, 128), width)

    def stage(i):
        hop = (i + 1) // 2
        odd = lax.rem(i, 2)
        block = ctx + hop - 2 * odd * hop
        return hop, 1 - odd, block, jnp.logical_and(block >= 0, block < ctx_size)

    def relay(way, hop, block, half):
        target = lax.rem(ctx + ctx_size + 1 - 2 * way, ctx_size)
        top = pl.multiple_of(block * width + half * (width // 2), 16)
        held = whole_out.at[pl.ds(top, width // 2), :]
        return describe(
            held,
            held,
            send_relay.at[2 * way + half, hop],
            recv_relay.at[2 * way + half, hop + 1],
            {"ctx": target, "tp": tp},
        )

    def can_relay(way):
        target = ctx + 1 - 2 * way
        return jnp.logical_and(target >= 0, target < ctx_size)

    whole_out[token_rows(ctx), :] = cotangent_ref[...]
    for half in range(2):
        for way in range(2):
            pl.when(can_relay(way))(lambda way=way, half=half: relay(way, 0, ctx, half).start())

    adapter_parts[0] = lax.dot_general(
        up_ref[...],
        cotangent_ref[...],
        (((1,), (1,)), ((), ())),
        preferred_element_type=jnp.float32,
    ).astype(jnp.bfloat16)
    adapter_copies = []
    for step in range(1, tp_size):
        device = {"ctx": ctx, "tp": lax.rem(tp + step, tp_size)}
        adapter_copies.append(
            push(
                adapter_parts.at[0],
                adapter_parts.at[step],
                send_ad.at[step],
                recv_ad.at[step],
                device,
            )
        )
    for copy in adapter_copies:
        copy.wait()
    adapter_total = adapter_parts[0].astype(jnp.float32)
    for step in range(1, tp_size):
        adapter_total += adapter_parts[step].astype(jnp.float32)
    adapter_sum[...] = adapter_total.astype(jnp.bfloat16)
    adapter_out[:, token_rows(ctx)] = adapter_sum[...]
    later = []
    for step in range(1, ctx_size):
        device = {"ctx": lax.rem(ctx + step, ctx_size), "tp": tp}
        later.append(
            push(
                adapter_sum,
                adapter_out.at[:, token_rows(ctx)],
                send_adsum.at[step],
                recv_adsum.at[step],
                device,
            )
        )

    def exchange(kind, src, dst, step):
        other = lax.rem(ctx + step, ctx_size)
        return describe(
            src.at[pl.ds(pl.multiple_of(other * ch_rows, 16), ch_rows), :],
            dst.at[:, token_rows(ctx)],
            send_row.at[kind, step],
            recv_row.at[kind, step],
            {"ctx": other, "tp": tp},
        )

    pairs = ((filter_ref, filter_out), (gated_ref, gated_out), (outer_ref, outer_out))
    my_rows = pl.ds(pl.multiple_of(ctx * ch_rows, 16), ch_rows)
    for src, dst in pairs:
        dst[:, token_rows(ctx)] = src[my_rows, :]

    def part_copy(block, step):
        other = lax.rem(tp + step, tp_size)
        return describe(
            partial.at[block, step],
            landed.at[block, step],
            send_part.at[block, step],
            recv_part.at[block, step],
            {"ctx": ctx, "tp": other},
        )

    place = ctx * tp_size + tp
    goal_ctx, goal_tp = lax.rem(place, ctx_size), place // ctx_size
    stays = jnp.logical_and(goal_ctx == ctx, goal_tp == tp)

    def sum_copy(block):
        return describe(
            summed.at[block],
            back_out.at[:, token_rows(block)],
            send_sum.at[block],
            recv_sum.at[block],
            {"ctx": goal_ctx, "tp": goal_tp},
        )

    def multiply(block):
        for step in list(range(1, tp_size)) + [0]:
            other = lax.rem(tp + step, tp_size)
            partial[block, step] = lax.dot_general(
                weight_ref[pl.ds(pl.multiple_of(other * rows, 16), rows), :],
                whole_out[token_rows(block), :],
                (((1,), (1,)), ((), ())),
                preferred_element_type=jnp.float32,
            ).astype(jnp.bfloat16)
            if step:
                part_copy(block, step).start()

    def finish(i):
        hop, way, block, valid = stage(i)

        @pl.when(valid)
        def _():
            total = partial[block, 0].astype(jnp.float32)
            for step in range(1, tp_size):
                part_copy(block, step).wait_recv()
                total += landed[block, step].astype(jnp.float32)
            summed[block] = total.astype(jnp.bfloat16)

            @pl.when(stays)
            def _():
                back_out[:, token_rows(block)] = summed[block]

            @pl.when(jnp.logical_not(stays))
            def _():
                sum_copy(block).start()

    def pass_on(side, hop, half):
        block = ctx - hop if side == 0 else ctx + hop

        @pl.when(jnp.logical_and(block >= 0, block < ctx_size))
        def _():
            relay(side, hop - 1, block, half).wait_recv()

            @pl.when(can_relay(side))
            def _():
                relay(side, hop, block, half).start()

    def body(i, carry):
        hop, way, block, valid = stage(i)

        @pl.when(way == 0)
        def _():
            for half in range(2):
                for side in range(2):
                    pass_on(side, hop, half)

        pl.when(valid)(lambda: multiply(block))

        @pl.when(i == exchange_step)
        def _():
            for kind, (src, dst) in enumerate(pairs):
                for step in range(1, ctx_size):
                    exchange(kind, src, dst, step).start()

        pl.when(i > 0)(lambda: finish(i - 1))
        return carry

    load.wait()
    lax.fori_loop(0, steps, body, 0)
    store = pltpu.make_async_copy(whole_out, whole_any, store_sem)
    store.start()
    finish(steps - 1)

    for way in range(2):
        for hop in range(ctx_size - 1):
            block = ctx - hop if way == 0 else ctx + hop
            held = jnp.logical_and(block >= 0, block < ctx_size)
            for half in range(2):
                pl.when(jnp.logical_and(held, can_relay(way)))(
                    lambda way=way, hop=hop, block=block, half=half: relay(
                        way, hop, block, half
                    ).wait_send()
                )
    for block in range(ctx_size):
        for step in range(1, tp_size):
            part_copy(block, step).wait_send()
    for copy in later:
        copy.wait()
    for kind, (src, dst) in enumerate(pairs):
        for step in range(1, ctx_size):
            exchange(kind, src, dst, step).wait()

    @pl.when(jnp.logical_not(stays))
    def _():
        for block in range(ctx_size):
            sum_copy(block).wait()

    store.wait()


def project_all(cotangent, weight, up_factor, masked_filter, gated, outer_gate):
    ctx_size, tp_size = lax.axis_size("ctx"), lax.axis_size("tp")
    width, features = cotangent.shape
    length = width * ctx_size
    rows = weight.shape[0] // tp_size
    rank = up_factor.shape[0]
    channels = jax.ShapeDtypeStruct((gated.shape[0] // ctx_size, length), jnp.bfloat16)
    dma = pltpu.SemaphoreType.DMA
    return pl.pallas_call(
        functools.partial(project_kernel, ctx_size, tp_size),
        out_shape=(
            jax.ShapeDtypeStruct((length, features), jnp.bfloat16),
            channels,
            channels,
            channels,
            jax.ShapeDtypeStruct((rows, length), jnp.bfloat16),
            jax.ShapeDtypeStruct((rank, length), jnp.bfloat16),
        ),
        in_specs=[
            pl.BlockSpec(memory_space=pl.ANY if arg == 1 else pltpu.VMEM) for arg in range(6)
        ],
        out_specs=tuple(
            pl.BlockSpec(memory_space=pl.ANY if out == 0 else pltpu.VMEM) for out in range(6)
        ),
        scratch_shapes=[
            pltpu.VMEM((ctx_size, tp_size, rows, width), jnp.bfloat16),
            pltpu.VMEM((ctx_size, tp_size, rows, width), jnp.bfloat16),
            pltpu.VMEM((ctx_size, rows, width), jnp.bfloat16),
            pltpu.VMEM((tp_size, rank, width), jnp.bfloat16),
            pltpu.VMEM((rank, width), jnp.bfloat16),
            dma((4, ctx_size)),
            dma((4, ctx_size)),
            dma((ctx_size, tp_size)),
            dma((ctx_size, tp_size)),
            dma((ctx_size,)),
            dma((ctx_size,)),
            dma((3, ctx_size)),
            dma((3, ctx_size)),
            dma((tp_size,)),
            dma((tp_size,)),
            dma((ctx_size,)),
            dma((ctx_size,)),
            pltpu.VMEM(weight.shape, jnp.bfloat16),
            pltpu.VMEM((length, features), jnp.bfloat16),
            dma,
            dma,
        ],
        compiler_params=pltpu.CompilerParams(
            collective_id=2, has_side_effects=True, vmem_limit_bytes=48 << 20
        ),
    )(cotangent, weight, up_factor, masked_filter, gated, outer_gate)


def token_by_kernel(count, shape, rank):
    return count <= kernel_peers and shape[1] <= dense_length and rank * shape[1] == count * 2048


def local(
    inner_gate_proj,
    outer_gate_proj,
    value_projection,
    channel_filter_lags,
    channel_filter_length,
    output_cotangent,
    output_weight,
    adapter_down_factor,
    adapter_up_factor,
):
    ctx_size, tp_size = lax.axis_size("ctx"), lax.axis_size("tp")
    tok_rows = inner_gate_proj.shape[1]
    lag_index = lax.axis_index("ctx") * tok_rows + lax.broadcasted_iota(
        jnp.int32, channel_filter_lags.shape, 1
    )
    masked_filter = jnp.where(
        lag_index < channel_filter_length[:, None],
        channel_filter_lags,
        jnp.zeros_like(channel_filter_lags),
    ).astype(jnp.bfloat16)
    gated = product_bf(inner_gate_proj, value_projection)
    by_kernel = token_by_kernel(
        ctx_size * tp_size,
        (gated.shape[0] // ctx_size, tok_rows * ctx_size),
        adapter_down_factor.shape[1],
    )
    if by_kernel:
        whole_cotangent, filter_ch, gated_ch, outer_ch, output_backward, adapter_t = project_all(
            output_cotangent,
            output_weight,
            adapter_up_factor,
            masked_filter,
            gated,
            outer_gate_proj,
        )
        output_backward = output_backward.astype(jnp.float32)
        adapter_backward = adapter_t.T
    else:
        whole_cotangent = lax.all_gather(output_cotangent, "ctx", axis=0, tiled=True)
        filter_ch, gated_ch, outer_ch = lax.all_to_all(
            jnp.stack([masked_filter, gated, outer_gate_proj]),
            "ctx",
            split_axis=1,
            concat_axis=2,
            tiled=True,
        )
        partial = lax.dot_general(
            output_weight,
            whole_cotangent,
            (((1,), (1,)), ((), ())),
            preferred_element_type=jnp.float32,
        ).astype(jnp.bfloat16)
        adapter_backward = lax.psum(
            lax.dot_general(
                whole_cotangent,
                adapter_up_factor,
                (((1,), (1,)), ((), ())),
                preferred_element_type=jnp.float32,
            ).astype(jnp.bfloat16),
            "tp",
        )
        scattered = lax.psum_scatter(partial, "tp", scatter_dimension=0, tiled=True)
        moves = [(i, (i % ctx_size) * tp_size + i // ctx_size) for i in range(ctx_size * tp_size)]
        output_backward = lax.ppermute(scattered, ("ctx", "tp"), moves).astype(jnp.float32)
    rows = filter_ch.shape[0]
    down_rows = lax.dynamic_slice_in_dim(
        adapter_down_factor, lax.axis_index("ctx") * rows, rows, axis=0
    )
    adapter_term = lax.dot_general(
        down_rows,
        adapter_backward,
        (((1,), (1,)), ((), ())),
        preferred_element_type=jnp.float32,
    )
    projected_gradient = (output_backward + adapter_term).astype(jnp.bfloat16)
    grad_conv = product_bf(projected_gradient, outer_ch)
    if filter_ch.shape[1] <= dense_length:
        conv_ch, grad_gated_ch = convolve_dense(filter_ch, gated_ch, grad_conv)
    else:
        conv_ch, grad_gated_ch = convolve(filter_ch.astype(jnp.float32), gated_ch, grad_conv)
    block_output = product_bf(outer_ch, conv_ch)
    outer_grad_ch = product_bf(projected_gradient, conv_ch)
    if by_kernel:
        token_t = lax.dot_general(
            down_rows,
            block_output,
            (((0,), (0,)), ((), ())),
            preferred_element_type=jnp.float32,
        ).astype(jnp.bfloat16)
        down_t = lax.dot_general(
            adapter_backward,
            block_output,
            (((0,), (1,)), ((), ())),
            preferred_element_type=jnp.float32,
        ).astype(jnp.bfloat16)
        grad_gated, outer_gate_gradient, down_sum, up_sum = return_all(
            grad_gated_ch, outer_grad_ch, token_t, down_t, whole_cotangent
        )
        return (
            product_bf(grad_gated, value_projection),
            outer_gate_gradient,
            product_bf(grad_gated, inner_gate_proj),
            down_sum.astype(jnp.float32).T * adapter_scale,
            up_sum,
        )
    token_part = lax.dot_general(
        block_output,
        down_rows,
        (((0,), (0,)), ((), ())),
        preferred_element_type=jnp.float32,
    )
    token_adapter = lax.psum(token_part.astype(jnp.bfloat16), ("ctx", "tp"))
    grad_gated, outer_gate_gradient = lax.all_to_all(
        jnp.stack([grad_gated_ch, outer_grad_ch]),
        "ctx",
        split_axis=2,
        concat_axis=1,
        tiled=True,
    )
    down_part = jnp.dot(block_output, adapter_backward, preferred_element_type=jnp.float32)
    down_sum = lax.all_gather(down_part.astype(jnp.bfloat16), "ctx", axis=0, tiled=True)
    up_sum = lax.dot_general(
        token_adapter,
        whole_cotangent,
        (((0,), (0,)), ((), ())),
        preferred_element_type=jnp.float32,
    )
    return (
        product_bf(grad_gated, value_projection),
        outer_gate_gradient,
        product_bf(grad_gated, inner_gate_proj),
        down_sum.astype(jnp.float32) * adapter_scale,
        up_sum * adapter_scale,
    )


def solution(mesh):
    return jax.shard_map(
        local,
        mesh=mesh,
        in_specs=(
            P("tp", ("groups", "ctx")),
            P("tp", ("groups", "ctx")),
            P("tp", ("groups", "ctx")),
            P("tp", "ctx"),
            P("tp"),
            P(("groups", "ctx"), "tp"),
            P("ctx", "tp"),
            P("tp", None),
            P(None, "tp"),
        ),
        out_specs=(
            P("tp", ("groups", "ctx")),
            P("tp", ("groups", "ctx")),
            P("tp", ("groups", "ctx")),
            P(("groups", "tp"), None),
            P("groups", "tp"),
        ),
        check_vma=False,
    )
```

```python
import functools
import math

import jax
import jax.numpy as jnp
import ml_dtypes
import numpy as np
from jax import lax
from jax.experimental import pallas as pl
from jax.experimental.pallas import tpu as pltpu
from jax.sharding import PartitionSpec as P

adapter_scale = 2.0


def product_bf(left, right):
    return (left.astype(jnp.float32) * right.astype(jnp.float32)).astype(jnp.bfloat16)


def dft_table(length):
    across = lax.broadcasted_iota(jnp.int32, (length, length), 0)
    downward = lax.broadcasted_iota(jnp.int32, (length, length), 1)
    angle = -2.0 * math.pi / length * (across * downward % length).astype(jnp.float32)
    return (jnp.cos(angle), jnp.sin(angle))


def twiddle_table(outer, inner):
    total = outer * inner
    first_idx = lax.broadcasted_iota(jnp.int32, (outer, inner), 0)
    second_idx = lax.broadcasted_iota(jnp.int32, (outer, inner), 1)
    angle = -2.0 * math.pi / total * (first_idx * second_idx % total).astype(jnp.float32)
    return (jnp.cos(angle), jnp.sin(angle))


def left_apply(table, field):
    return jnp.einsum("ap,cpq->caq", table, field, precision=lax.Precision.HIGHEST)


def right_apply(field, table):
    return jnp.einsum("caq,qb->cab", field, table, precision=lax.Precision.HIGHEST)


def forward_dft(signal, tables):
    outer_cos, outer_sin, inner_cos, inner_sin, twist_cos, twist_sin = tables
    channels = signal.shape[0]
    block = signal.reshape(channels, outer_cos.shape[0], inner_cos.shape[0])
    first_real = left_apply(outer_cos, block)
    first_imag = left_apply(outer_sin, block)
    turned_real = first_real * twist_cos - first_imag * twist_sin
    turned_imag = first_real * twist_sin + first_imag * twist_cos
    spec_real = right_apply(turned_real, inner_cos) - right_apply(turned_imag, inner_sin)
    spec_imag = right_apply(turned_real, inner_sin) + right_apply(turned_imag, inner_cos)
    return (spec_real, spec_imag)


def inverse_real(spec_real, spec_imag, tables):
    outer_cos, outer_sin, inner_cos, inner_sin, twist_cos, twist_sin = tables
    back_real = right_apply(spec_real, inner_cos) + right_apply(spec_imag, inner_sin)
    back_imag = right_apply(spec_imag, inner_cos) - right_apply(spec_real, inner_sin)
    untwist_real = back_real * twist_cos + back_imag * twist_sin
    untwist_imag = back_imag * twist_cos - back_real * twist_sin
    result = left_apply(outer_cos, untwist_real) + left_apply(outer_sin, untwist_imag)
    total = outer_cos.shape[0] * inner_cos.shape[0]
    return result.reshape(result.shape[0], total) / total


def convolve(taps, gated, grad_conv):
    channels, length = taps.shape
    total = 2 * length
    outer = 1 << (total.bit_length() - 1) // 2
    inner = total // outer
    outer_cos, outer_sin = dft_table(outer)
    inner_cos, inner_sin = dft_table(inner)
    twist_cos, twist_sin = twiddle_table(outer, inner)
    tables = (outer_cos, outer_sin, inner_cos, inner_sin, twist_cos, twist_sin)
    padding = jnp.zeros((channels, length), jnp.float32)

    def spectrum(field):
        return forward_dft(jnp.concatenate([field.astype(jnp.float32), padding], axis=1), tables)

    filt_real, filt_imag = spectrum(taps)
    gated_real, gated_imag = spectrum(gated)
    grad_real, grad_imag = spectrum(grad_conv)
    forward_val = inverse_real(
        filt_real * gated_real - filt_imag * gated_imag,
        filt_real * gated_imag + filt_imag * gated_real,
        tables,
    )[:, :length]
    backward_val = inverse_real(
        filt_real * grad_real + filt_imag * grad_imag,
        filt_real * grad_imag - filt_imag * grad_real,
        tables,
    )[:, :length]
    return (forward_val.astype(jnp.bfloat16), backward_val.astype(jnp.bfloat16))


dense_length = 2048


def dense_table(length):
    lag = np.arange(length, dtype=np.int64)[:, None]
    freq = np.arange(length, dtype=np.int64)[None, :]
    angle = np.pi / (2 * length) * (lag * (2 * freq + 1) % (4 * length))
    table = np.concatenate([np.cos(angle), np.sin(angle)], axis=1)
    return jnp.asarray(table.astype(ml_dtypes.bfloat16))


def dense_spectrum(field, table):
    spec = jnp.dot(field, table, preferred_element_type=jnp.float32)
    return spec[:, : field.shape[1]], spec[:, field.shape[1] :]


def dense_inverse(cos_part, sin_part, table):
    spec = jnp.concatenate([cos_part, sin_part], axis=1).astype(jnp.bfloat16)
    field = lax.dot_general(
        spec, table, (((1,), (1,)), ((), ())), preferred_element_type=jnp.float32
    )
    return (field * (1.0 / table.shape[0])).astype(jnp.bfloat16)


def convolve_dense(taps, gated, grad_conv):
    table = dense_table(taps.shape[1])
    filt_cos, filt_sin = dense_spectrum(taps, table)
    gated_cos, gated_sin = dense_spectrum(gated, table)
    conv = dense_inverse(
        filt_cos * gated_cos - filt_sin * gated_sin,
        filt_cos * gated_sin + filt_sin * gated_cos,
        table,
    )
    grad_cos, grad_sin = dense_spectrum(grad_conv, table)
    back = dense_inverse(
        filt_cos * grad_cos + filt_sin * grad_sin,
        filt_cos * grad_sin - filt_sin * grad_cos,
        table,
    )
    return conv, back


kernel_peers = 16


def position():
    ctx_size, tp_size = lax.axis_size("ctx"), lax.axis_size("tp")
    count = ctx_size * tp_size
    me = lax.axis_index("ctx") * tp_size + lax.axis_index("tp")

    def peer(step):
        other = lax.rem(me + step, count)
        return {"ctx": other // tp_size, "tp": lax.rem(other, tp_size)}

    return me, count, peer


def greet(count, peer):
    barrier = pltpu.get_barrier_semaphore()
    for step in range(1, count):
        pl.semaphore_signal(
            barrier, inc=1, device_id=peer(step), device_id_type=pl.DeviceIdType.MESH
        )
    pl.semaphore_wait(barrier, count - 1)


def push(src, dst, send_sem, recv_sem, device):
    copy = pltpu.make_async_remote_copy(
        src_ref=src,
        dst_ref=dst,
        send_sem=send_sem,
        recv_sem=recv_sem,
        device_id=device,
        device_id_type=pl.DeviceIdType.MESH,
    )
    copy.start()
    return copy


def return_kernel(
    ctx_size,
    tp_size,
    grad_ref,
    outer_ref,
    token_ref,
    down_ref,
    cotangent_any,
    grad_out,
    outer_out,
    down_out,
    up_out,
    parts,
    whole,
    send_tok,
    recv_tok,
    send_all,
    recv_all,
    send_row,
    recv_row,
    local_sem,
    cotangent_ref,
    load_sem,
):
    load = pltpu.make_async_copy(cotangent_any, cotangent_ref, load_sem)
    load.start()
    me, count, peer = position()
    ctx, tp = lax.axis_index("ctx"), lax.axis_index("tp")
    rows, length = grad_ref.shape
    width = length // ctx_size
    lanes = length // 128
    greet(count, peer)

    def chunk(ref, place):
        top = pl.multiple_of(place // lanes * 16, 16)
        left = pl.multiple_of(lax.rem(place, lanes) * 128, 128)
        return ref.at[pl.ds(top, 16), pl.ds(left, 128)]

    copies = []
    for step in range(1, count):
        copies.append(
            push(
                chunk(token_ref, lax.rem(me + step, count)),
                parts.at[step],
                send_tok.at[step],
                recv_tok.at[step],
                peer(step),
            )
        )
    my_rows = pl.ds(pl.multiple_of(ctx * rows, 16), rows)
    my_cols = pl.ds(pl.multiple_of(ctx * width, 128), width)
    my_lags = pl.ds(pl.multiple_of(ctx * rows, 128), rows)
    later = []
    for step in range(1, ctx_size):
        other = lax.rem(ctx + step, ctx_size)
        device = {"ctx": other, "tp": tp}
        cols = pl.ds(pl.multiple_of(other * width, 128), width)
        moves = (
            (down_ref, down_out.at[:, my_lags]),
            (grad_ref.at[:, cols], grad_out.at[my_rows, :]),
            (outer_ref.at[:, cols], outer_out.at[my_rows, :]),
        )
        for kind, (src, dst) in enumerate(moves):
            later.append(push(src, dst, send_row.at[kind, step], recv_row.at[kind, step], device))
    down_out[:, my_lags] = down_ref[...]
    grad_out[my_rows, :] = grad_ref[:, my_cols]
    outer_out[my_rows, :] = outer_ref[:, my_cols]

    own = pltpu.make_async_copy(chunk(token_ref, me), parts.at[0], local_sem)
    own.start()
    own.wait()
    total = parts[0].astype(jnp.float32)
    for step in range(1, count):
        copies[step - 1].wait_recv()
        total += parts[step].astype(jnp.float32)
    for copy in copies:
        copy.wait_send()
    parts[0] = total.astype(jnp.bfloat16)
    copies = []
    for step in range(1, count):
        copies.append(
            push(
                parts.at[0],
                chunk(whole, me),
                send_all.at[step],
                recv_all.at[step],
                peer(step),
            )
        )
    own = pltpu.make_async_copy(parts.at[0], chunk(whole, me), local_sem)
    own.start()
    own.wait()
    for copy in copies:
        copy.wait()
    load.wait()
    up_out[...] = adapter_scale * jnp.dot(
        whole[...], cotangent_ref[...], preferred_element_type=jnp.float32
    )
    for copy in later:
        copy.wait()


def return_all(grad_gated_ch, outer_grad_ch, token_t, down_t, whole_cotangent):
    ctx_size, tp_size = lax.axis_size("ctx"), lax.axis_size("tp")
    count = ctx_size * tp_size
    rows, length = grad_gated_ch.shape
    rank = token_t.shape[0]
    tokens = jax.ShapeDtypeStruct((rows * ctx_size, length // ctx_size), jnp.bfloat16)
    dma = pltpu.SemaphoreType.DMA
    return pl.pallas_call(
        functools.partial(return_kernel, ctx_size, tp_size),
        out_shape=(
            tokens,
            tokens,
            jax.ShapeDtypeStruct((rank, rows * ctx_size), jnp.bfloat16),
            jax.ShapeDtypeStruct((rank, whole_cotangent.shape[1]), jnp.float32),
        ),
        in_specs=[pl.BlockSpec(memory_space=pltpu.VMEM)] * 4
        + [pl.BlockSpec(memory_space=pl.ANY)],
        out_specs=(pl.BlockSpec(memory_space=pltpu.VMEM),) * 4,
        scratch_shapes=[
            pltpu.VMEM((count, 16, 128), jnp.bfloat16),
            pltpu.VMEM((rank, length), jnp.bfloat16),
            dma((count,)),
            dma((count,)),
            dma((count,)),
            dma((count,)),
            dma((3, ctx_size)),
            dma((3, ctx_size)),
            dma,
            pltpu.VMEM(whole_cotangent.shape, jnp.bfloat16),
            dma,
        ],
        compiler_params=pltpu.CompilerParams(
            collective_id=1, has_side_effects=True, vmem_limit_bytes=40 << 20
        ),
    )(grad_gated_ch, outer_grad_ch, token_t, down_t, whole_cotangent)


exchange_step = 2


def project_kernel(
    ctx_size,
    tp_size,
    cotangent_ref,
    weight_any,
    up_ref,
    filter_ref,
    gated_ref,
    outer_ref,
    whole_any,
    filter_out,
    gated_out,
    outer_out,
    back_out,
    adapter_out,
    partial,
    landed,
    summed,
    adapter_parts,
    adapter_sum,
    send_relay,
    recv_relay,
    send_part,
    recv_part,
    send_sum,
    recv_sum,
    send_row,
    recv_row,
    send_ad,
    recv_ad,
    send_adsum,
    recv_adsum,
    weight_ref,
    whole_out,
    load_sem,
    store_sem,
):
    load = pltpu.make_async_copy(weight_any, weight_ref, load_sem)
    load.start()
    me, count, peer = position()
    ctx, tp = lax.axis_index("ctx"), lax.axis_index("tp")
    width = cotangent_ref.shape[0]
    rows = weight_ref.shape[0] // tp_size
    ch_rows = filter_out.shape[0]
    steps = 2 * (ctx_size - 1) + 1
    greet(count, peer)

    def describe(src, dst, send_sem, recv_sem, device):
        return pltpu.make_async_remote_copy(
            src_ref=src,
            dst_ref=dst,
            send_sem=send_sem,
            recv_sem=recv_sem,
            device_id=device,
            device_id_type=pl.DeviceIdType.MESH,
        )

    def token_rows(block):
        return pl.ds(pl.multiple_of(block * width, 128), width)

    def stage(i):
        hop = (i + 1) // 2
        odd = lax.rem(i, 2)
        block = ctx + hop - 2 * odd * hop
        return hop, 1 - odd, block, jnp.logical_and(block >= 0, block < ctx_size)

    def relay(way, hop, block, half):
        target = lax.rem(ctx + ctx_size + 1 - 2 * way, ctx_size)
        top = pl.multiple_of(block * width + half * (width // 2), 16)
        held = whole_out.at[pl.ds(top, width // 2), :]
        return describe(
            held,
            held,
            send_relay.at[2 * way + half, hop],
            recv_relay.at[2 * way + half, hop + 1],
            {"ctx": target, "tp": tp},
        )

    def can_relay(way):
        target = ctx + 1 - 2 * way
        return jnp.logical_and(target >= 0, target < ctx_size)

    whole_out[token_rows(ctx), :] = cotangent_ref[...]
    for half in range(2):
        for way in range(2):
            pl.when(can_relay(way))(lambda way=way, half=half: relay(way, 0, ctx, half).start())

    adapter_parts[0] = lax.dot_general(
        up_ref[...],
        cotangent_ref[...],
        (((1,), (1,)), ((), ())),
        preferred_element_type=jnp.float32,
    ).astype(jnp.bfloat16)
    adapter_copies = []
    for step in range(1, tp_size):
        device = {"ctx": ctx, "tp": lax.rem(tp + step, tp_size)}
        adapter_copies.append(
            push(
                adapter_parts.at[0],
                adapter_parts.at[step],
                send_ad.at[step],
                recv_ad.at[step],
                device,
            )
        )
    for copy in adapter_copies:
        copy.wait()
    adapter_total = adapter_parts[0].astype(jnp.float32)
    for step in range(1, tp_size):
        adapter_total += adapter_parts[step].astype(jnp.float32)
    adapter_sum[...] = adapter_total.astype(jnp.bfloat16)
    adapter_out[:, token_rows(ctx)] = adapter_sum[...]
    later = []
    for step in range(1, ctx_size):
        device = {"ctx": lax.rem(ctx + step, ctx_size), "tp": tp}
        later.append(
            push(
                adapter_sum,
                adapter_out.at[:, token_rows(ctx)],
                send_adsum.at[step],
                recv_adsum.at[step],
                device,
            )
        )

    def exchange(kind, src, dst, step):
        other = lax.rem(ctx + step, ctx_size)
        return describe(
            src.at[pl.ds(pl.multiple_of(other * ch_rows, 16), ch_rows), :],
            dst.at[:, token_rows(ctx)],
            send_row.at[kind, step],
            recv_row.at[kind, step],
            {"ctx": other, "tp": tp},
        )

    pairs = ((filter_ref, filter_out), (gated_ref, gated_out), (outer_ref, outer_out))
    my_rows = pl.ds(pl.multiple_of(ctx * ch_rows, 16), ch_rows)
    for src, dst in pairs:
        dst[:, token_rows(ctx)] = src[my_rows, :]

    def part_copy(block, step):
        other = lax.rem(tp + step, tp_size)
        return describe(
            partial.at[block, step],
            landed.at[block, step],
            send_part.at[block, step],
            recv_part.at[block, step],
            {"ctx": ctx, "tp": other},
        )

    place = ctx * tp_size + tp
    goal_ctx, goal_tp = lax.rem(place, ctx_size), place // ctx_size
    stays = jnp.logical_and(goal_ctx == ctx, goal_tp == tp)

    def sum_copy(block):
        return describe(
            summed.at[block],
            back_out.at[:, token_rows(block)],
            send_sum.at[block],
            recv_sum.at[block],
            {"ctx": goal_ctx, "tp": goal_tp},
        )

    def multiply(block):
        for step in list(range(1, tp_size)) + [0]:
            other = lax.rem(tp + step, tp_size)
            partial[block, step] = lax.dot_general(
                weight_ref[pl.ds(pl.multiple_of(other * rows, 16), rows), :],
                whole_out[token_rows(block), :],
                (((1,), (1,)), ((), ())),
                preferred_element_type=jnp.float32,
            ).astype(jnp.bfloat16)
            if step:
                part_copy(block, step).start()

    def finish(i):
        hop, way, block, valid = stage(i)

        @pl.when(valid)
        def _():
            total = partial[block, 0].astype(jnp.float32)
            for step in range(1, tp_size):
                part_copy(block, step).wait_recv()
                total += landed[block, step].astype(jnp.float32)
            summed[block] = total.astype(jnp.bfloat16)

            @pl.when(stays)
            def _():
                back_out[:, token_rows(block)] = summed[block]

            @pl.when(jnp.logical_not(stays))
            def _():
                sum_copy(block).start()

    def pass_on(side, hop, half):
        block = ctx - hop if side == 0 else ctx + hop

        @pl.when(jnp.logical_and(block >= 0, block < ctx_size))
        def _():
            relay(side, hop - 1, block, half).wait_recv()

            @pl.when(can_relay(side))
            def _():
                relay(side, hop, block, half).start()

    def body(i, carry):
        hop, way, block, valid = stage(i)

        @pl.when(way == 0)
        def _():
            for half in range(2):
                for side in range(2):
                    pass_on(side, hop, half)

        pl.when(valid)(lambda: multiply(block))

        @pl.when(i == exchange_step)
        def _():
            for kind, (src, dst) in enumerate(pairs):
                for step in range(1, ctx_size):
                    exchange(kind, src, dst, step).start()

        pl.when(i > 0)(lambda: finish(i - 1))
        return carry

    load.wait()
    lax.fori_loop(0, steps, body, 0)
    store = pltpu.make_async_copy(whole_out, whole_any, store_sem)
    store.start()
    finish(steps - 1)

    for way in range(2):
        for hop in range(ctx_size - 1):
            block = ctx - hop if way == 0 else ctx + hop
            held = jnp.logical_and(block >= 0, block < ctx_size)
            for half in range(2):
                pl.when(jnp.logical_and(held, can_relay(way)))(
                    lambda way=way, hop=hop, block=block, half=half: relay(
                        way, hop, block, half
                    ).wait_send()
                )
    for block in range(ctx_size):
        for step in range(1, tp_size):
            part_copy(block, step).wait_send()
    for copy in later:
        copy.wait()
    for kind, (src, dst) in enumerate(pairs):
        for step in range(1, ctx_size):
            exchange(kind, src, dst, step).wait()

    @pl.when(jnp.logical_not(stays))
    def _():
        for block in range(ctx_size):
            sum_copy(block).wait()

    store.wait()


def project_all(cotangent, weight, up_factor, masked_filter, gated, outer_gate):
    ctx_size, tp_size = lax.axis_size("ctx"), lax.axis_size("tp")
    width, features = cotangent.shape
    length = width * ctx_size
    rows = weight.shape[0] // tp_size
    rank = up_factor.shape[0]
    channels = jax.ShapeDtypeStruct((gated.shape[0] // ctx_size, length), jnp.bfloat16)
    dma = pltpu.SemaphoreType.DMA
    return pl.pallas_call(
        functools.partial(project_kernel, ctx_size, tp_size),
        out_shape=(
            jax.ShapeDtypeStruct((length, features), jnp.bfloat16),
            channels,
            channels,
            channels,
            jax.ShapeDtypeStruct((rows, length), jnp.bfloat16),
            jax.ShapeDtypeStruct((rank, length), jnp.bfloat16),
        ),
        in_specs=[
            pl.BlockSpec(memory_space=pl.ANY if arg == 1 else pltpu.VMEM) for arg in range(6)
        ],
        out_specs=tuple(
            pl.BlockSpec(memory_space=pl.ANY if out == 0 else pltpu.VMEM) for out in range(6)
        ),
        scratch_shapes=[
            pltpu.VMEM((ctx_size, tp_size, rows, width), jnp.bfloat16),
            pltpu.VMEM((ctx_size, tp_size, rows, width), jnp.bfloat16),
            pltpu.VMEM((ctx_size, rows, width), jnp.bfloat16),
            pltpu.VMEM((tp_size, rank, width), jnp.bfloat16),
            pltpu.VMEM((rank, width), jnp.bfloat16),
            dma((4, ctx_size)),
            dma((4, ctx_size)),
            dma((ctx_size, tp_size)),
            dma((ctx_size, tp_size)),
            dma((ctx_size,)),
            dma((ctx_size,)),
            dma((3, ctx_size)),
            dma((3, ctx_size)),
            dma((tp_size,)),
            dma((tp_size,)),
            dma((ctx_size,)),
            dma((ctx_size,)),
            pltpu.VMEM(weight.shape, jnp.bfloat16),
            pltpu.VMEM((length, features), jnp.bfloat16),
            dma,
            dma,
        ],
        compiler_params=pltpu.CompilerParams(
            collective_id=2, has_side_effects=True, vmem_limit_bytes=48 << 20
        ),
    )(cotangent, weight, up_factor, masked_filter, gated, outer_gate)


def token_by_kernel(count, shape, rank):
    return count <= kernel_peers and shape[1] <= dense_length and rank * shape[1] == count * 2048


def local(
    inner_gate_proj,
    outer_gate_proj,
    value_projection,
    channel_filter_lags,
    channel_filter_length,
    output_cotangent,
    output_weight,
    adapter_down_factor,
    adapter_up_factor,
):
    ctx_size, tp_size = lax.axis_size("ctx"), lax.axis_size("tp")
    tok_rows = inner_gate_proj.shape[1]
    lag_index = lax.axis_index("ctx") * tok_rows + lax.broadcasted_iota(
        jnp.int32, channel_filter_lags.shape, 1
    )
    masked_filter = jnp.where(
        lag_index < channel_filter_length[:, None],
        channel_filter_lags,
        jnp.zeros_like(channel_filter_lags),
    ).astype(jnp.bfloat16)
    gated = product_bf(inner_gate_proj, value_projection)
    by_kernel = token_by_kernel(
        ctx_size * tp_size,
        (gated.shape[0] // ctx_size, tok_rows * ctx_size),
        adapter_down_factor.shape[1],
    )
    if by_kernel:
        whole_cotangent, filter_ch, gated_ch, outer_ch, output_backward, adapter_t = project_all(
            output_cotangent,
            output_weight,
            adapter_up_factor,
            masked_filter,
            gated,
            outer_gate_proj,
        )
        output_backward = output_backward.astype(jnp.float32)
        adapter_backward = adapter_t.T
    else:
        whole_cotangent = lax.all_gather(output_cotangent, "ctx", axis=0, tiled=True)
        filter_ch, gated_ch, outer_ch = lax.all_to_all(
            jnp.stack([masked_filter, gated, outer_gate_proj]),
            "ctx",
            split_axis=1,
            concat_axis=2,
            tiled=True,
        )
        partial = lax.dot_general(
            output_weight,
            whole_cotangent,
            (((1,), (1,)), ((), ())),
            preferred_element_type=jnp.float32,
        ).astype(jnp.bfloat16)
        adapter_backward = lax.psum(
            lax.dot_general(
                whole_cotangent,
                adapter_up_factor,
                (((1,), (1,)), ((), ())),
                preferred_element_type=jnp.float32,
            ).astype(jnp.bfloat16),
            "tp",
        )
        scattered = lax.psum_scatter(partial, "tp", scatter_dimension=0, tiled=True)
        moves = [(i, (i % ctx_size) * tp_size + i // ctx_size) for i in range(ctx_size * tp_size)]
        output_backward = lax.ppermute(scattered, ("ctx", "tp"), moves).astype(jnp.float32)
    rows = filter_ch.shape[0]
    down_rows = lax.dynamic_slice_in_dim(
        adapter_down_factor, lax.axis_index("ctx") * rows, rows, axis=0
    )
    adapter_term = lax.dot_general(
        down_rows,
        adapter_backward,
        (((1,), (1,)), ((), ())),
        preferred_element_type=jnp.float32,
    )
    projected_gradient = (output_backward + adapter_term).astype(jnp.bfloat16)
    grad_conv = product_bf(projected_gradient, outer_ch)
    if filter_ch.shape[1] <= dense_length:
        conv_ch, grad_gated_ch = convolve_dense(filter_ch, gated_ch, grad_conv)
    else:
        conv_ch, grad_gated_ch = convolve(filter_ch.astype(jnp.float32), gated_ch, grad_conv)
    block_output = product_bf(outer_ch, conv_ch)
    outer_grad_ch = product_bf(projected_gradient, conv_ch)
    if by_kernel:
        token_t = lax.dot_general(
            down_rows,
            block_output,
            (((0,), (0,)), ((), ())),
            preferred_element_type=jnp.float32,
        ).astype(jnp.bfloat16)
        down_t = lax.dot_general(
            adapter_backward,
            block_output,
            (((0,), (1,)), ((), ())),
            preferred_element_type=jnp.float32,
        ).astype(jnp.bfloat16)
        grad_gated, outer_gate_gradient, down_sum, up_sum = return_all(
            grad_gated_ch, outer_grad_ch, token_t, down_t, whole_cotangent
        )
        return (
            product_bf(grad_gated, value_projection),
            outer_gate_gradient,
            product_bf(grad_gated, inner_gate_proj),
            down_sum.astype(jnp.float32).T * adapter_scale,
            up_sum,
        )
    token_part = lax.dot_general(
        block_output,
        down_rows,
        (((0,), (0,)), ((), ())),
        preferred_element_type=jnp.float32,
    )
    token_adapter = lax.psum(token_part.astype(jnp.bfloat16), ("ctx", "tp"))
    grad_gated, outer_gate_gradient = lax.all_to_all(
        jnp.stack([grad_gated_ch, outer_grad_ch]),
        "ctx",
        split_axis=2,
        concat_axis=1,
        tiled=True,
    )
    down_part = jnp.dot(block_output, adapter_backward, preferred_element_type=jnp.float32)
    down_sum = lax.all_gather(down_part.astype(jnp.bfloat16), "ctx", axis=0, tiled=True)
    up_sum = lax.dot_general(
        token_adapter,
        whole_cotangent,
        (((0,), (0,)), ((), ())),
        preferred_element_type=jnp.float32,
    )
    return (
        product_bf(grad_gated, value_projection),
        outer_gate_gradient,
        product_bf(grad_gated, inner_gate_proj),
        down_sum.astype(jnp.float32) * adapter_scale,
        up_sum * adapter_scale,
    )


def solution(mesh):
    return jax.shard_map(
        local,
        mesh=mesh,
        in_specs=(
            P("tp", ("groups", "ctx")),
            P("tp", ("groups", "ctx")),
            P("tp", ("groups", "ctx")),
            P("tp", "ctx"),
            P("tp"),
            P(("groups", "ctx"), "tp"),
            P("ctx", "tp"),
            P("tp", None),
            P(None, "tp"),
        ),
        out_specs=(
            P("tp", ("groups", "ctx")),
            P("tp", ("groups", "ctx")),
            P("tp", ("groups", "ctx")),
            P(("groups", "tp"), None),
            P("groups", "tp"),
        ),
        check_vma=False,
    )
```
